512 devices in a mesh: outer: 16 (over z, y_hi), inner: 32 (over y_lo, x, core).
Axes of the slice: x: 4, y: 8 (y_hi: 2, y_lo: 4; y = y_hi * 4 + y_lo), z: 8, core: 2. Of those that a mesh axis runs over, the one named last changes fastest.
Arguments:
- image_embed: bfloat16 [65536, 768], P(('outer', 'inner')), may hold values from -0.21582031 to 0.21582031
- text_embed: bfloat16 [8192, 768], P(('outer', 'inner')), may hold values from -0.21582031 to 0.21582031
- log_scale: float32 [1], replicated, may hold values from 0.7 to 2.3
- logit_bias: float32 [1], replicated, may hold values from -4 to -1
- pair_index: int32 [8192], P(('outer', 'inner')), may hold values from 0 to 65535, as said below
Outputs:
- image_grad: bfloat16 [65536, 768], P(('outer', 'inner'))
- text_grad: bfloat16 [8192, 768], P(('outer', 'inner'))
The draws below stay inside these ranges and needn't reach their ends.
Inputs may be any that keep to these rules, and one draw needn't show every extreme that they name: `pair_index`: no two text rows are paired with the same image row; images 0 and 65535 are always paired.
All inputs are finite; a program needn't handle non-finite values.
Results may differ from the reference program's by a relative error of at most 0.009.
Values may be sent and summed in bfloat16 or wider, within the bound.
No kernel may reach another device: no remote copies, remote signals or barrier semaphores. Data moves between devices by JAX's collectives and lax.ppermute only.
A program may use at most 64 MiB of HBM per device.

```python
import jax
import jax.numpy as jnp
from jax import lax

D = 768
BATCH = 65536
TEXTS = 8192


def draw_pair_index(key, part):
    key = jax.random.fold_in(key, 7)
    shuffled = jax.random.permutation(key, BATCH).astype(jnp.int32)
    chosen = shuffled[:TEXTS]
    chosen = jnp.where(chosen == jnp.max(chosen), jnp.int32(BATCH - 1), chosen)
    chosen = jnp.where(chosen == jnp.min(chosen), jnp.int32(0), chosen)
    return chosen.astype(jnp.int32)


def steps_of(key, extent, cuts, smallest, high):
    def one(dim, blocks):
        draws = jax.random.uniform(jax.random.fold_in(jax.random.fold_in(key, 6), dim), (blocks,), jnp.float32, smallest / len(cuts), high / len(cuts))
        return jnp.repeat(jnp.exp(draws), extent[dim] // blocks).reshape((-1,) + (1,) * (len(extent) - dim - 1))

    gain = one(*cuts[0])
    for cut in cuts[1:]:
        gain = gain * one(*cut)
    return gain


def gaussian(key, extent, spread, reach, shards=(), kind=jnp.bfloat16):
    gain = steps_of(key, extent, shards, -0.22, 0.18) if shards else 1.0
    values = jax.random.normal(key, extent, jnp.float32) * spread * gain
    return jnp.minimum(jnp.maximum(values, -reach), reach).astype(kind)


def setup_inputs(seed: int = 0) -> dict:
    keys = jax.random.split(jax.random.key(seed), 6)
    image_embed = gaussian(keys[0], (BATCH, D), (D ** -0.5), 0.21582031, ((0, 512),))
    text_embed = gaussian(keys[1], (TEXTS, D), (D ** -0.5), 0.21582031, ((0, 512),))
    log_scale = jnp.clip(jax.random.uniform(keys[2], (1,), jnp.float32, 0.7, 2.3), 0.7, 2.3)
    logit_bias = jnp.clip(jax.random.uniform(keys[3], (1,), jnp.float32, -4.0, -1.0), -4.0, -1.0)
    pair_index = draw_pair_index(jax.random.fold_in(keys[5], 71), 0)
    return dict(image_embed=image_embed, text_embed=text_embed, log_scale=log_scale, logit_bias=logit_bias, pair_index=pair_index)


def normalize(values):
    floats = values.astype(jnp.float32)
    inverse = lax.rsqrt(lax.optimization_barrier(jnp.sum(floats * floats, axis=-1, keepdims=True)) + 1e-06)
    return (floats * inverse, inverse)

def unit_backward(floats, inverse, grad):
    along = lax.optimization_barrier(jnp.sum(floats * grad, axis=-1, keepdims=True))
    return ((grad - floats * along) * inverse).astype(jnp.bfloat16)

def reference(image_embed, text_embed, log_scale, logit_bias, pair_index):
    image_float, image_inverse = normalize(image_embed)
    text_float, text_inverse = normalize(text_embed)
    image_unit = image_float.astype(jnp.bfloat16)
    text_unit = text_float.astype(jnp.bfloat16)
    scale = jnp.exp(log_scale[0])
    offset = logit_bias[0]
    total_rows = image_embed.shape[0]
    block = min(total_rows, 4096)
    while total_rows % block != 0:
        block = block // 2
    count = total_rows // block
    image_blocks = image_unit.reshape(count, block, image_unit.shape[1])
    one = jnp.float32(1.0)

    def step(text_total, item):
        index, images = item
        rows_all = index * block + jnp.arange(block, dtype=jnp.int32)
        logits = scale * jnp.dot(images, text_unit.T, preferred_element_type=jnp.float32) + offset
        label = jnp.where(pair_index[None, :] == rows_all[:, None], one, -one)
        weight = (-label * jax.nn.sigmoid(-label * logits) * scale).astype(jnp.bfloat16)
        image_part = jnp.dot(weight, text_unit, preferred_element_type=jnp.float32)
        text_total = text_total + jnp.dot(weight.T, images, preferred_element_type=jnp.float32)
        return (text_total, image_part)
    start = jnp.zeros(text_unit.shape, jnp.float32)
    text_unit_grad, image_parts = lax.scan(step, start, (jnp.arange(count, dtype=jnp.int32), image_blocks))
    image_unit_grad = image_parts.reshape(total_rows, image_unit.shape[1])
    return (unit_backward(image_float, image_inverse, image_unit_grad), unit_backward(text_float, text_inverse, text_unit_grad))
```

```python
import functools

import jax
import jax.numpy as jnp
from jax import lax
from jax.experimental import pallas as pl
from jax.experimental.pallas import tpu as pltpu
from jax.sharding import Mesh
from jax.sharding import PartitionSpec as P

AXES = ("z", "yh", "yl", "x", "c")
TEXT_AXES = ("z", "yh", "yl")
IMAGE_AXES = ("x", "c")
LANES = 128


def normalize(values):
    floats = values.astype(jnp.float32)
    inverse = lax.rsqrt(jnp.sum(floats * floats, axis=-1, keepdims=True) + 1e-06)
    return (floats * inverse, inverse)


def unit_backward(floats, inverse, grad):
    along = jnp.sum(floats * grad, axis=-1, keepdims=True)
    return ((grad - floats * along) * inverse).astype(jnp.bfloat16)


def pair_kernel(first_ref, scalars_ref, image_ref, text_ref, pair_ref, image_grad_ref, text_grad_ref, text_acc):
    step = pl.program_id(0)
    block = image_ref.shape[0]
    scale = scalars_ref[0]
    offset = scalars_ref[1]
    images = image_ref[...]
    texts = text_ref[...]
    dots = lax.dot_general(images, texts, (((1,), (1,)), ((), ())), preferred_element_type=jnp.float32)
    chance = 1.0 / (1.0 + jnp.exp(-(scale * dots + offset)))
    rows = first_ref[0] + step * block + lax.broadcasted_iota(jnp.int32, chance.shape, 0)
    paired = pair_ref[...] == rows
    weight = (scale * jnp.where(paired, chance - 1.0, chance)).astype(jnp.bfloat16)
    image_grad_ref[...] = jnp.dot(weight, texts, preferred_element_type=jnp.float32).astype(image_grad_ref.dtype)
    term = lax.dot_general(weight, images, (((0,), (0,)), ((), ())), preferred_element_type=jnp.float32)

    @pl.when(step == 0)
    def _():
        text_acc[...] = term

    @pl.when(step > 0)
    def _():
        text_acc[...] += term

    @pl.when(step == pl.num_programs(0) - 1)
    def _():
        text_grad_ref[...] = text_acc[...].astype(text_grad_ref.dtype)


def pair_block(first, scalars, images, texts, pairs, block):
    rows, width = images.shape
    count = texts.shape[0]
    return pl.pallas_call(
        pair_kernel,
        grid=(rows // block,),
        in_specs=[
            pl.BlockSpec(memory_space=pltpu.SMEM),
            pl.BlockSpec(memory_space=pltpu.SMEM),
            pl.BlockSpec((block, width), lambda i: (i, 0)),
            pl.BlockSpec((count, width), lambda i: (0, 0)),
            pl.BlockSpec((1, count), lambda i: (0, 0)),
        ],
        out_specs=[
            pl.BlockSpec((block, width), lambda i: (i, 0)),
            pl.BlockSpec((count, width), lambda i: (0, 0)),
        ],
        out_shape=[
            jax.ShapeDtypeStruct((rows, width), jnp.bfloat16),
            jax.ShapeDtypeStruct((count, width), jnp.bfloat16),
        ],
        scratch_shapes=[pltpu.VMEM((count, width), jnp.float32)],
        compiler_params=pltpu.CompilerParams(vmem_limit_bytes=40 * 1024 * 1024),
        cost_estimate=pl.CostEstimate(
            flops=6 * rows * count * width, bytes_accessed=8 * (rows + count) * width, transcendentals=2 * rows * count
        ),
    )(first, scalars, images, texts, pairs)


def on_device(image_embed, text_embed, log_scale, logit_bias, pair_index):
    own_images, width = image_embed.shape
    own_texts = text_embed.shape[0]
    peers = lax.axis_size(TEXT_AXES)
    members = lax.axis_size(IMAGE_AXES)
    image_float, image_inverse = normalize(image_embed)
    text_float, text_inverse = normalize(text_embed)
    scalars = jnp.concatenate([jnp.exp(log_scale), logit_bias])

    images = lax.all_gather(image_float.astype(jnp.bfloat16), IMAGE_AXES, axis=0, tiled=True)

    lane = lax.broadcasted_iota(jnp.int32, (own_texts, LANES), 1)
    digits = jnp.where(lane == 0, pair_index[:, None] // 256, jnp.where(lane == 1, pair_index[:, None] % 256, 0))
    packet = jnp.concatenate([text_float.astype(jnp.bfloat16), digits.astype(jnp.bfloat16)], axis=1)
    spread = jnp.broadcast_to(packet[None], (peers, own_texts, width + LANES))
    gathered = lax.all_to_all(spread, TEXT_AXES, split_axis=0, concat_axis=0, tiled=True)
    gathered = gathered.reshape(peers * own_texts, width + LANES)
    texts = gathered[:, :width]
    pairs = gathered[:, width].astype(jnp.int32) * 256 + gathered[:, width + 1].astype(jnp.int32)

    first = lax.axis_index(TEXT_AXES) * (own_images * members)
    image_part, text_part = pair_block(
        jnp.reshape(first, (1,)).astype(jnp.int32), scalars, images, texts, pairs[None, :], 256
    )
    image_total = lax.psum_scatter(image_part, IMAGE_AXES, scatter_dimension=0, tiled=True)
    text_parts = lax.all_to_all(
        text_part.reshape(peers, own_texts, width), TEXT_AXES, split_axis=0, concat_axis=0, tiled=True
    )
    text_total = jnp.sum(text_parts.astype(jnp.float32), axis=0)
    return (
        unit_backward(image_float, image_inverse, image_total.astype(jnp.float32)),
        unit_backward(text_float, text_inverse, text_total),
    )


def solution(mesh):
    split = Mesh(mesh.devices.reshape(8, 2, 4, 4, 2), AXES)
    rows = P(AXES, None)
    return jax.shard_map(
        on_device,
        mesh=split,
        in_specs=(rows, rows, P(), P(), P(AXES)),
        out_specs=(rows, rows),
        check_vma=False,
    )
```

```python
import jax
import jax.numpy as jnp
from jax import lax
from jax.experimental import pallas as pl
from jax.experimental.pallas import tpu as pltpu
from jax.sharding import Mesh
from jax.sharding import PartitionSpec as P

AXES = ("z", "yh", "yl", "x", "c")
FAR = ("z", "yh")
LANES = 128
BLOCK = 256
VMEM = 40 * 1024 * 1024


def normalize(values):
    floats = values.astype(jnp.float32)
    inverse = lax.rsqrt(jnp.sum(floats * floats, axis=-1, keepdims=True) + 1e-06)
    return (floats * inverse, inverse)


def unit_backward(floats, inverse, grad):
    along = jnp.sum(floats * grad, axis=-1, keepdims=True)
    return ((grad - floats * along) * inverse).astype(jnp.bfloat16)


def shifted(array, axis, by):
    devices = lax.axis_size(axis)
    return lax.ppermute(array, axis, [(i, (i + by) % devices) for i in range(devices)])


def chunk_kernel(first_ref, scalars_ref, own_ref, other_ref, packet_ref, weight_ref, grad_ref):
    width = own_ref.shape[1]
    scale = scalars_ref[0]
    offset = scalars_ref[1]
    texts = packet_ref[:, :width]
    digits = packet_ref[:, width:].astype(jnp.float32).T
    pairs = (digits[0:1] * 256.0 + digits[1:2]).astype(jnp.int32)
    half = own_ref.shape[0]
    pieces = BLOCK // 128
    total = None
    for block in range(2 * half // BLOCK):
        source, start = (own_ref, block * BLOCK) if block * BLOCK < half else (other_ref, block * BLOCK - half)
        images = source[start : start + BLOCK, :]
        dots = lax.dot_general(images, texts, (((1,), (1,)), ((), ())), preferred_element_type=jnp.float32)
        chance = 1.0 / (1.0 + jnp.exp(-(scale * dots + offset)))
        row = lax.broadcasted_iota(jnp.int32, (128, 1), 0)
        rows = jnp.concatenate([row + first_ref[block * pieces + p] for p in range(pieces)], axis=0)
        weight = (scale * jnp.where(pairs == rows, chance - 1.0, chance)).astype(jnp.bfloat16)
        weight_ref[block * BLOCK : (block + 1) * BLOCK, :] = weight
        term = lax.dot_general(weight, images, (((0,), (0,)), ((), ())), preferred_element_type=jnp.float32)
        total = term if total is None else total + term
    grad_ref[...] = total.astype(grad_ref.dtype)


def chunk_terms(first, scalars, own, other, packet, grad_type):
    half, width = own.shape
    count = packet.shape[0]
    smem = pl.BlockSpec(memory_space=pltpu.SMEM)
    vmem = pl.BlockSpec(memory_space=pltpu.VMEM)
    return pl.pallas_call(
        chunk_kernel,
        in_specs=[smem, smem, vmem, vmem, vmem],
        out_specs=[vmem, vmem],
        out_shape=[
            jax.ShapeDtypeStruct((2 * half, count), jnp.bfloat16),
            jax.ShapeDtypeStruct((count, width), grad_type),
        ],
        compiler_params=pltpu.CompilerParams(vmem_limit_bytes=VMEM),
        cost_estimate=pl.CostEstimate(
            flops=8 * half * count * width,
            bytes_accessed=4 * half * (width + count) + 4 * count * width,
            transcendentals=4 * half * count,
        ),
    )(first, scalars, own, other, packet)


def image_kernel(start, *refs):
    weights, packets, out_ref = refs[:4], refs[4:8], refs[8]
    width = out_ref.shape[1]
    for block in range(out_ref.shape[0] // BLOCK):
        total = None
        for weight_ref, packet_ref in zip(weights, packets):
            weight = weight_ref[start + block * BLOCK : start + (block + 1) * BLOCK, :]
            term = jnp.dot(weight, packet_ref[:, :width], preferred_element_type=jnp.float32)
            total = term if total is None else total + term
        out_ref[block * BLOCK : (block + 1) * BLOCK, :] = total.astype(out_ref.dtype)


def image_terms(weights, packets, start, half, width, out_type):
    vmem = pl.BlockSpec(memory_space=pltpu.VMEM)
    count = packets[0].shape[0]
    return pl.pallas_call(
        lambda *refs: image_kernel(start, *refs),
        in_specs=[vmem] * 8,
        out_specs=vmem,
        out_shape=jax.ShapeDtypeStruct((half, width), out_type),
        compiler_params=pltpu.CompilerParams(vmem_limit_bytes=VMEM),
        cost_estimate=pl.CostEstimate(
            flops=8 * half * count * width, bytes_accessed=16 * half * count + 8 * count * width, transcendentals=0
        ),
    )(*weights, *packets)


def on_device(image_embed, text_embed, log_scale, logit_bias, pair_index):
    own_images, width = image_embed.shape
    own_texts = text_embed.shape[0]
    peers = lax.axis_size(FAR)
    near = lax.axis_size("yl")
    ring = lax.axis_size("x")
    image_float, image_inverse = normalize(image_embed)
    text_float, text_inverse = normalize(text_embed)
    scalars = jnp.concatenate([jnp.exp(log_scale), logit_bias])

    lane = lax.broadcasted_iota(jnp.int32, (own_texts, LANES), 1)
    digits = jnp.where(lane == 0, pair_index[:, None] // 256, jnp.where(lane == 1, pair_index[:, None] % 256, 0))
    packet = jnp.concatenate([text_float.astype(jnp.bfloat16), digits.astype(jnp.bfloat16)], axis=1)
    spread = jnp.broadcast_to(packet[None], (peers, own_texts, width + LANES))
    packet = lax.all_to_all(spread, FAR, split_axis=0, concat_axis=0, tiled=True)
    packet = packet.reshape(peers * own_texts, width + LANES)

    image_unit = image_float.astype(jnp.bfloat16)
    own = jnp.concatenate([image_unit] + [shifted(image_unit, "yl", s) for s in range(1, near)], axis=0)
    other = shifted(own, "c", 1)

    far_id, yl, x, c = lax.axis_index(FAR), lax.axis_index("yl"), lax.axis_index("x"), lax.axis_index("c")
    group = lax.axis_size("x") * lax.axis_size("c")
    first = jnp.stack(
        [
            (((far_id * near + (yl - s) % near) * group) + x * 2 + core) * own_images
            for core in (c, 1 - c)
            for s in range(near)
        ]
    ).astype(jnp.int32)

    order = (0, 1, ring - 1, 2)
    packets = [packet] + [shifted(packet, "x", s) for s in order[1:]]
    weights, text_total = [], None
    for step, chunk in zip(order, packets):
        weight, part = chunk_terms(first, scalars, own, other, chunk, jnp.float32 if step == 0 else jnp.bfloat16)
        weights.append(weight)
        part = part if step == 0 else shifted(part, "x", -step).astype(jnp.float32)
        text_total = part if text_total is None else text_total + part

    half = near * own_images
    other_part = image_terms(weights, packets, half, half, width, jnp.bfloat16)
    own_part = image_terms(weights, packets, 0, half, width, jnp.float32)
    image_part = own_part + shifted(other_part, "c", 1).astype(jnp.float32)
    image_total = image_part[:own_images]
    for s in range(1, near):
        sent = image_part[s * own_images : (s + 1) * own_images].astype(jnp.bfloat16)
        image_total = image_total + shifted(sent, "yl", -s).astype(jnp.float32)

    text_parts = lax.all_to_all(
        text_total.astype(jnp.bfloat16).reshape(peers, own_texts, width), FAR, split_axis=0, concat_axis=0, tiled=True
    )
    text_own = jnp.sum(text_parts.astype(jnp.float32), axis=0)
    return (
        unit_backward(image_float, image_inverse, image_total),
        unit_backward(text_float, text_inverse, text_own),
    )


def solution(mesh):
    split = Mesh(mesh.devices.reshape(8, 2, 4, 4, 2), AXES)
    rows = P(AXES, None)
    return jax.shard_map(
        on_device,
        mesh=split,
        in_specs=(rows, rows, P(), P(), P(AXES)),
        out_specs=(rows, rows),
        check_vma=False,
    )
```

```python
import math

import jax
import jax.numpy as jnp
from jax import lax
from jax.experimental import pallas as pl
from jax.experimental.pallas import tpu as pltpu
from jax.sharding import Mesh
from jax.sharding import PartitionSpec as P

AXES = ("z", "y", "x", "c")
SIZES = (8, 8, 4, 2)
LANES = 128
BLOCK = 256
VMEM = 40 * 1024 * 1024


def normalize(values):
    floats = values.astype(jnp.float32)
    inverse = lax.rsqrt(jnp.sum(floats * floats, axis=-1, keepdims=True) + 1e-06)
    return (floats * inverse, inverse)


def unit_backward(floats, inverse, grad):
    along = jnp.sum(floats * grad, axis=-1, keepdims=True)
    return ((grad - floats * along) * inverse).astype(jnp.bfloat16)


def image_rings():
    depth, length, width, cores = SIZES
    rings = []
    for z in range(depth):
        for x in range(width):
            for c in range(cores):
                ring = [((z * length + y) * width + x) * cores + c for y in range(length)]
                rings.append(ring if c == 0 else ring[::-1])
    return rings


def exchanged(array):
    return lax.ppermute(array, "c", [(0, 1), (1, 0)])


def spread(rows, axis):
    peers = lax.axis_size(axis)
    copies = jnp.broadcast_to(rows[None], (peers,) + rows.shape)
    return lax.all_to_all(copies, axis, split_axis=0, concat_axis=0, tiled=True).reshape(-1, rows.shape[1])


def summed(rows, axis):
    peers = lax.axis_size(axis)
    parts = rows.reshape(peers, -1, rows.shape[1])
    parts = lax.all_to_all(parts, axis, split_axis=0, concat_axis=0, tiled=True)
    return jnp.sum(parts.astype(jnp.float32), axis=0)


def weight_kernel(first_ref, scalars_ref, image_ref, own_ref, other_ref, weight_ref, grad_ref, pairs_ref):
    step = pl.program_id(0)
    width = image_ref.shape[1]
    count = own_ref.shape[0]
    halves = (own_ref, other_ref)

    @pl.when(step == 0)
    def _():
        for i, ref in enumerate(halves):
            digits = ref[:, width:].astype(jnp.float32).T
            pairs_ref[:, i * count : (i + 1) * count] = (digits[0:1] * 256.0 + digits[1:2]).astype(jnp.int32)

    scale = scalars_ref[0]
    slope = scalars_ref[1]
    shift = scalars_ref[2]
    images = image_ref[...]
    pieces = BLOCK // 128
    row = lax.broadcasted_iota(jnp.int32, (128, 1), 0)
    rows = jnp.concatenate([row + first_ref[step * pieces + p] for p in range(pieces)], axis=0)
    grad = None
    for i, ref in enumerate(halves):
        texts = ref[:, :width]
        dots = lax.dot_general(images, texts, (((1,), (1,)), ((), ())), preferred_element_type=jnp.float32)
        chance = 1.0 / (1.0 + jnp.exp2(dots * slope + shift))
        paired = pairs_ref[:, i * count : (i + 1) * count] == rows
        weight = (scale * jnp.where(paired, chance - 1.0, chance)).astype(jnp.bfloat16)
        weight_ref[:, i * count : (i + 1) * count] = weight
        term = jnp.dot(weight, texts, preferred_element_type=jnp.float32)
        grad = term if grad is None else grad + term
    grad_ref[...] = grad.astype(grad_ref.dtype)


def weights_and_image_terms(first, scalars, images, own, other):
    rows, width = images.shape
    count, wide = own.shape
    smem = pl.BlockSpec(memory_space=pltpu.SMEM)
    return pl.pallas_call(
        weight_kernel,
        grid=(rows // BLOCK,),
        in_specs=[
            smem,
            smem,
            pl.BlockSpec((BLOCK, width), lambda i: (i, 0)),
            pl.BlockSpec((count, wide), lambda i: (0, 0)),
            pl.BlockSpec((count, wide), lambda i: (0, 0)),
        ],
        out_specs=[
            pl.BlockSpec((BLOCK, 2 * count), lambda i: (i, 0)),
            pl.BlockSpec((BLOCK, width), lambda i: (i, 0)),
        ],
        out_shape=[
            jax.ShapeDtypeStruct((rows, 2 * count), jnp.bfloat16),
            jax.ShapeDtypeStruct((rows, width), jnp.bfloat16),
        ],
        scratch_shapes=[pltpu.VMEM((1, 2 * count), jnp.int32)],
        compiler_params=pltpu.CompilerParams(vmem_limit_bytes=VMEM),
        cost_estimate=pl.CostEstimate(
            flops=8 * rows * count * width,
            bytes_accessed=4 * rows * (width + count) + 4 * count * wide,
            transcendentals=4 * rows * count,
        ),
    )(first, scalars, images, own, other)


def text_kernel(weight_ref, image_ref, grad_ref, total_ref):
    step = pl.program_id(0)
    term = lax.dot_general(
        weight_ref[...], image_ref[...], (((0,), (0,)), ((), ())), preferred_element_type=jnp.float32
    )

    @pl.when(step == 0)
    def _():
        total_ref[...] = term

    @pl.when(step > 0)
    def _():
        total_ref[...] += term

    @pl.when(step == pl.num_programs(0) - 1)
    def _():
        grad_ref[...] = total_ref[...].astype(grad_ref.dtype)


def text_terms(weights, images, half, out_type):
    rows, width = images.shape
    count = weights.shape[1] // 2
    return pl.pallas_call(
        text_kernel,
        grid=(rows // BLOCK,),
        in_specs=[
            pl.BlockSpec((BLOCK, count), lambda i: (i, half)),
            pl.BlockSpec((BLOCK, width), lambda i: (i, 0)),
        ],
        out_specs=pl.BlockSpec((count, width), lambda i: (0, 0)),
        out_shape=jax.ShapeDtypeStruct((count, width), out_type),
        scratch_shapes=[pltpu.VMEM((count, width), jnp.float32)],
        compiler_params=pltpu.CompilerParams(vmem_limit_bytes=VMEM),
        cost_estimate=pl.CostEstimate(
            flops=2 * rows * count * width, bytes_accessed=2 * rows * (width + count) + 2 * count * width, transcendentals=0
        ),
    )(weights, images)


def on_device(image_embed, text_embed, log_scale, logit_bias, pair_index):
    own_images, width = image_embed.shape
    own_texts = text_embed.shape[0]
    rings = image_rings()
    image_float, image_inverse = normalize(image_embed)
    images = lax.all_gather(image_float.astype(jnp.bfloat16), AXES, axis=0, tiled=True, axis_index_groups=rings)

    text_float, text_inverse = normalize(text_embed)
    lane = lax.broadcasted_iota(jnp.int32, (own_texts, LANES), 1)
    digits = jnp.where(lane == 0, pair_index[:, None] // 256, jnp.where(lane == 1, pair_index[:, None] % 256, 0))
    packet = jnp.concatenate([text_float.astype(jnp.bfloat16), digits.astype(jnp.bfloat16)], axis=1)
    own = spread(spread(packet, "z"), "x")
    other = exchanged(own)

    scale = jnp.exp(log_scale)
    scalars = jnp.concatenate([scale, -math.log2(math.e) * scale, -math.log2(math.e) * logit_bias])
    z, x, c = lax.axis_index("z"), lax.axis_index("x"), lax.axis_index("c")
    place = jnp.arange(SIZES[1], dtype=jnp.int32)
    place = jnp.where(c == 0, place, SIZES[1] - 1 - place)
    first = (((z * SIZES[1] + place) * SIZES[2] + x) * SIZES[3] + c) * own_images

    weights, image_part = weights_and_image_terms(first.astype(jnp.int32), scalars, images, own, other)
    image_total = lax.psum_scatter(image_part, AXES, scatter_dimension=0, tiled=True, axis_index_groups=rings)

    other_part = exchanged(text_terms(weights, images, 1, jnp.bfloat16))
    text_part = text_terms(weights, images, 0, jnp.float32) + other_part.astype(jnp.float32)
    text_part = summed(text_part.astype(jnp.bfloat16), "x")
    text_total = summed(text_part.astype(jnp.bfloat16), "z")
    return (
        unit_backward(image_float, image_inverse, image_total.astype(jnp.float32)),
        unit_backward(text_float, text_inverse, text_total),
    )


def solution(mesh):
    split = Mesh(mesh.devices.reshape(SIZES), AXES)
    rows = P(AXES, None)
    return jax.shard_map(
        on_device,
        mesh=split,
        in_specs=(rows, rows, P(), P(), P(AXES)),
        out_specs=(rows, rows),
        check_vma=False,
    )
```

```python
import math

import jax
import jax.numpy as jnp
from jax import lax
from jax.experimental import pallas as pl
from jax.experimental.pallas import tpu as pltpu
from jax.sharding import Mesh
from jax.sharding import PartitionSpec as P

AXES = ("z", "yh", "ym", "yl", "x", "c")
SIZES = (8, 2, 2, 2, 4, 2)
FAR = ("z", "yh", "ym")
LANES = 128
BLOCK = 256
VMEM = 56 * 1024 * 1024
ROWS_BY_ROWS = (((1,), (1,)), ((), ()))
COLUMNS_BY_ROWS = (((0,), (0,)), ((), ()))

smem = pl.BlockSpec(memory_space=pltpu.SMEM)
vmem = pl.BlockSpec(memory_space=pltpu.VMEM)


def params():
    return pltpu.CompilerParams(vmem_limit_bytes=VMEM)


def shifted(array, axis, by):
    devices = lax.axis_size(axis)
    return lax.ppermute(array, axis, [(i, (i + by) % devices) for i in range(devices)])


def inverse_norm(floats):
    return lax.rsqrt(jnp.sum(floats * floats, axis=-1, keepdims=True) + 1e-06)


def image_unit_kernel(embed_ref, unit_ref):
    floats = embed_ref[...].astype(jnp.float32)
    unit_ref[...] = (floats * inverse_norm(floats)).astype(unit_ref.dtype)


def image_units(embed):
    return pl.pallas_call(
        image_unit_kernel,
        in_specs=[vmem],
        out_specs=vmem,
        out_shape=jax.ShapeDtypeStruct(embed.shape, jnp.bfloat16),
        compiler_params=params(),
    )(embed)


def packet_kernel(pair_ref, embed_ref, packet_ref):
    rows, width = embed_ref.shape
    floats = embed_ref[...].astype(jnp.float32)
    unit = (floats * inverse_norm(floats)).astype(packet_ref.dtype)
    row = lax.broadcasted_iota(jnp.int32, (rows, LANES), 0)
    lane = lax.broadcasted_iota(jnp.int32, (rows, LANES), 1)
    index = jnp.zeros((rows, LANES), jnp.int32)
    for i in range(rows):
        index = jnp.where(row == i, pair_ref[i], index)
    digits = jnp.where(lane == 0, index >> 8, jnp.where(lane == 1, index & 255, 0))
    digits = digits.astype(jnp.float32).astype(packet_ref.dtype)
    for peer in range(packet_ref.shape[0]):
        packet_ref[peer, :, :width] = unit
        packet_ref[peer, :, width:] = digits


def text_packets(pair_index, embed, peers):
    rows, width = embed.shape
    return pl.pallas_call(
        packet_kernel,
        in_specs=[smem, vmem],
        out_specs=vmem,
        out_shape=jax.ShapeDtypeStruct((peers, rows, width + LANES), jnp.bfloat16),
        compiler_params=params(),
    )(pair_index, embed)


def block_weights(first_ref, scalars_ref, images, texts, pairs):
    pieces = BLOCK // 128
    start = pl.program_id(0) * pieces
    row = lax.broadcasted_iota(jnp.int32, (128, 1), 0)
    rows = jnp.concatenate([row + first_ref[start + p] for p in range(pieces)], axis=0)
    dots = lax.dot_general(images, texts, ROWS_BY_ROWS, preferred_element_type=jnp.float32)
    chance = 1.0 / (1.0 + jnp.exp2(dots * scalars_ref[1] + scalars_ref[2]))
    return (scalars_ref[0] * jnp.where(pairs == rows, chance - 1.0, chance)).astype(jnp.bfloat16)


def weight_kernel(first_ref, scalars_ref, image_ref, packet_ref, weight_ref, *rest):
    pairs_ref = rest[-1]
    step = pl.program_id(0)
    width = image_ref.shape[1]

    @pl.when(step == 0)
    def _():
        digits = packet_ref[:, width:].astype(jnp.float32).T
        pairs_ref[...] = (digits[0:1] * 256.0 + digits[1:2]).astype(jnp.int32)

    images = image_ref[...]
    weight = block_weights(first_ref, scalars_ref, images, packet_ref[:, :width], pairs_ref[...])
    weight_ref[...] = weight
    if len(rest) > 1:
        grad_ref, total_ref = rest[:2]
        add_up(step, total_ref, lax.dot_general(weight, images, COLUMNS_BY_ROWS, preferred_element_type=jnp.float32))

        @pl.when(step == pl.num_programs(0) - 1)
        def _():
            grad_ref[...] = total_ref[...].astype(grad_ref.dtype)


def add_up(step, total_ref, term):
    @pl.when(step == 0)
    def _():
        total_ref[...] = term

    @pl.when(step > 0)
    def _():
        total_ref[...] += term


def pair_weights(first, scalars, images, packet, with_grad):
    rows, width = images.shape
    count, wide = packet.shape
    out_specs = [pl.BlockSpec((BLOCK, count), lambda i: (i, 0))]
    out_shape = [jax.ShapeDtypeStruct((rows, count), jnp.bfloat16)]
    scratch = [pltpu.VMEM((1, count), jnp.int32)]
    if with_grad:
        out_specs.append(pl.BlockSpec((count, width), lambda i: (0, 0)))
        out_shape.append(jax.ShapeDtypeStruct((count, width), jnp.bfloat16))
        scratch.insert(0, pltpu.VMEM((count, width), jnp.float32))
    return pl.pallas_call(
        weight_kernel,
        grid=(rows // BLOCK,),
        in_specs=[
            smem,
            smem,
            pl.BlockSpec((BLOCK, width), lambda i: (i, 0)),
            pl.BlockSpec((count, wide), lambda i: (0, 0)),
        ],
        out_specs=out_specs,
        out_shape=out_shape,
        scratch_shapes=scratch,
        compiler_params=params(),
        cost_estimate=pl.CostEstimate(
            flops=(4 if with_grad else 2) * rows * count * width,
            bytes_accessed=2 * rows * (width + count) + 2 * count * wide,
            transcendentals=2 * rows * count,
        ),
    )(first, scalars, images, packet)


def grad_kernel(own_weight_ref, other_weight_ref, image_ref, own_ref, other_ref, text_grad_ref, *rest):
    image_grad_refs, total_ref = rest[:-1], rest[-1]
    step = pl.program_id(0)
    width = image_ref.shape[1]
    weight = own_weight_ref[...]
    add_up(
        step, total_ref, lax.dot_general(weight, image_ref[...], COLUMNS_BY_ROWS, preferred_element_type=jnp.float32)
    )
    term = jnp.dot(weight, own_ref[:, :width], preferred_element_type=jnp.float32)
    term += jnp.dot(other_weight_ref[...], other_ref[:, :width], preferred_element_type=jnp.float32)
    for i, ref in enumerate(image_grad_refs):

        @pl.when(step == i)
        def _():
            ref[...] = term.astype(ref.dtype)

    @pl.when(step == pl.num_programs(0) - 1)
    def _():
        text_grad_ref[...] = total_ref[...]


def grad_terms(own_weight, other_weight, images, own, other):
    rows, width = images.shape
    count, wide = own.shape
    steps = rows // BLOCK
    rolling = pl.BlockSpec((BLOCK, count), lambda i: (i, 0))
    whole = pl.BlockSpec((count, wide), lambda i: (0, 0))
    return pl.pallas_call(
        grad_kernel,
        grid=(steps,),
        in_specs=[rolling, rolling, pl.BlockSpec((BLOCK, width), lambda i: (i, 0)), whole, whole],
        out_specs=[pl.BlockSpec((count, width), lambda i: (0, 0))]
        + [pl.BlockSpec((BLOCK, width), lambda i: (0, 0))] * steps,
        out_shape=[jax.ShapeDtypeStruct((count, width), jnp.float32)]
        + [jax.ShapeDtypeStruct((BLOCK, width), jnp.bfloat16)] * steps,
        scratch_shapes=[pltpu.VMEM((count, width), jnp.float32)],
        compiler_params=params(),
        cost_estimate=pl.CostEstimate(
            flops=6 * rows * count * width,
            bytes_accessed=4 * rows * (width + count) + 8 * count * wide,
            transcendentals=0,
        ),
    )(own_weight, other_weight, images, own, other)


def backward_kernel(embed_ref, *refs):
    floats = embed_ref[...].astype(jnp.float32)
    inverse = inverse_norm(floats)
    unit = floats * inverse
    parts_refs, out_ref = refs[:-1], refs[-1]
    grad = None
    for ref in parts_refs:
        parts = [ref[i] for i in range(ref.shape[0])] if len(ref.shape) == 3 else [ref[...]]
        for part in parts:
            part = part.astype(jnp.float32)
            grad = part if grad is None else grad + part
    along = jnp.sum(unit * grad, axis=-1, keepdims=True)
    out_ref[...] = ((grad - unit * along) * inverse).astype(out_ref.dtype)


def unit_backward(embed, *parts):
    return pl.pallas_call(
        backward_kernel,
        in_specs=[vmem] * (1 + len(parts)),
        out_specs=vmem,
        out_shape=jax.ShapeDtypeStruct(embed.shape, jnp.bfloat16),
        compiler_params=params(),
    )(embed, *parts)


def on_device(image_embed, text_embed, log_scale, logit_bias, pair_index):
    own_images, width = image_embed.shape
    own_texts = text_embed.shape[0]
    peers = lax.axis_size(FAR)
    ring = lax.axis_size("x")

    unit = image_units(image_embed)
    pair = jnp.concatenate([unit, shifted(unit, "yl", 1)], axis=0)
    packets = text_packets(pair_index, text_embed, peers)
    own = lax.all_to_all(packets, FAR, split_axis=0, concat_axis=0, tiled=True)
    own = own.reshape(peers * own_texts, width + LANES)
    other = shifted(own, "c", 1)
    images = jnp.concatenate([pair] + [shifted(pair, "x", s) for s in range(1, ring)], axis=0)

    scale = jnp.exp(log_scale)
    scalars = jnp.concatenate([scale, -math.log2(math.e) * scale, -math.log2(math.e) * logit_bias])
    far, yl, x, c = lax.axis_index(FAR), lax.axis_index("yl"), lax.axis_index("x"), lax.axis_index("c")
    first = jnp.stack(
        [
            (((far * 2 + place) * ring + (x - s) % ring) * 2 + c) * own_images
            for s in range(ring)
            for place in (yl, 1 - yl)
        ]
    ).astype(jnp.int32)

    (own_weight,) = pair_weights(first, scalars, images, own, False)
    other_weight, other_part = pair_weights(first, scalars, images, other, True)
    own_part, *image_parts = grad_terms(own_weight, other_weight, images, own, other)

    text_part = (own_part + shifted(other_part, "c", 1).astype(jnp.float32)).astype(jnp.bfloat16)
    text_parts = lax.all_to_all(
        text_part.reshape(peers, own_texts, width), FAR, split_axis=0, concat_axis=0, tiled=True
    )

    image_total = image_parts[0].astype(jnp.float32)
    for s in range(1, ring):
        image_total = image_total + shifted(image_parts[s], "x", -s).astype(jnp.float32)
    beside = shifted(image_total[own_images:].astype(jnp.bfloat16), "yl", 1)
    return (
        unit_backward(image_embed, image_total[:own_images], beside),
        unit_backward(text_embed, text_parts),
    )


def solution(mesh):
    split = Mesh(mesh.devices.reshape(SIZES), AXES)
    rows = P(AXES, None)
    return jax.shard_map(
        on_device,
        mesh=split,
        in_specs=(rows, rows, P(), P(), P(AXES)),
        out_specs=(rows, rows),
        check_vma=False,
    )
```

```python
import math

import jax
import jax.numpy as jnp
from jax import lax
from jax.experimental import pallas as pl
from jax.experimental.pallas import tpu as pltpu
from jax.sharding import Mesh
from jax.sharding import PartitionSpec as P

AXES = ("z", "yh", "ym", "yl", "x", "c")
SIZES = (8, 2, 2, 2, 4, 2)
FAR = ("z", "yh", "ym")
MIDDLE = ("yh", "ym")
LANES = 128
VMEM = 56 * 1024 * 1024
ROWS_BY_ROWS = (((1,), (1,)), ((), ()))
COLUMNS_BY_ROWS = (((0,), (0,)), ((), ()))

smem = pl.BlockSpec(memory_space=pltpu.SMEM)
vmem = pl.BlockSpec(memory_space=pltpu.VMEM)


def params():
    return pltpu.CompilerParams(vmem_limit_bytes=VMEM)


def shifted(array, axis, by):
    devices = lax.axis_size(axis)
    return lax.ppermute(array, axis, [(i, (i + by) % devices) for i in range(devices)])


def inverse_norm(floats):
    return lax.rsqrt(jnp.sum(floats * floats, axis=-1, keepdims=True) + 1e-06)


def unit_kernel(pair_ref, image_ref, text_ref, unit_ref, packet_ref):
    floats = image_ref[...].astype(jnp.float32)
    unit_ref[...] = (floats * inverse_norm(floats)).astype(unit_ref.dtype)
    rows, width = text_ref.shape
    floats = text_ref[...].astype(jnp.float32)
    unit = (floats * inverse_norm(floats)).astype(packet_ref.dtype)
    row = lax.broadcasted_iota(jnp.int32, (rows, LANES), 0)
    lane = lax.broadcasted_iota(jnp.int32, (rows, LANES), 1)
    index = jnp.zeros((rows, LANES), jnp.int32)
    for i in range(rows):
        index = jnp.where(row == i, pair_ref[i], index)
    digits = jnp.where(lane == 0, index >> 8, jnp.where(lane == 1, index & 255, 0))
    digits = digits.astype(jnp.float32).astype(packet_ref.dtype)
    for peer in range(packet_ref.shape[0]):
        packet_ref[peer, :, :width] = unit
        packet_ref[peer, :, width:] = digits


def units_and_packets(pair_index, image_embed, text_embed, peers):
    rows, width = text_embed.shape
    return pl.pallas_call(
        unit_kernel,
        in_specs=[smem, vmem, vmem],
        out_specs=[vmem, vmem],
        out_shape=[
            jax.ShapeDtypeStruct(image_embed.shape, jnp.bfloat16),
            jax.ShapeDtypeStruct((peers, rows, width + LANES), jnp.bfloat16),
        ],
        compiler_params=params(),
    )(pair_index, image_embed, text_embed)


def pair_kernel(chunks, first_ref, scalars_ref, *refs):
    chunk_refs, packet_refs = refs[:chunks], refs[chunks : chunks + 2]
    text_grad_refs = refs[chunks + 2 : chunks + 4]
    image_grad_refs = refs[chunks + 4 : 2 * chunks + 4]
    image_ref, text_ref, sems = refs[2 * chunks + 4 :]
    block, width = chunk_refs[0].shape
    count = packet_refs[0].shape[0]
    copies = [
        pltpu.make_async_copy(ref, image_ref.at[pl.ds(i * block, block)], sems.at[i]) for i, ref in enumerate(chunk_refs)
    ]
    copies += [
        pltpu.make_async_copy(ref, text_ref.at[pl.ds(i * count, count)], sems.at[chunks + i])
        for i, ref in enumerate(packet_refs)
    ]
    for copy in copies:
        copy.start()
    for copy in copies:
        copy.wait()

    digits = text_ref[:, width:].astype(jnp.float32).T
    pairs = (digits[0:1] * 256.0 + digits[1:2]).astype(jnp.int32)
    row = lax.broadcasted_iota(jnp.int32, (128, 1), 0)
    rows = jnp.concatenate([row + first_ref[p] for p in range(chunks * block // 128)], axis=0)
    images = image_ref[...]
    texts = text_ref[:, :width]
    dots = lax.dot_general(images, texts, ROWS_BY_ROWS, preferred_element_type=jnp.float32)
    chance = 1.0 / (1.0 + jnp.exp2(dots * scalars_ref[1] + scalars_ref[2]))
    weight = (scalars_ref[0] * jnp.where(pairs == rows, chance - 1.0, chance)).astype(jnp.bfloat16)
    text_grad = lax.dot_general(weight, images, COLUMNS_BY_ROWS, preferred_element_type=jnp.float32)
    for i, ref in enumerate(text_grad_refs):
        ref[...] = text_grad[i * count : (i + 1) * count].astype(ref.dtype)
    image_grad = jnp.dot(weight, texts, preferred_element_type=jnp.float32)
    for i, ref in enumerate(image_grad_refs):
        ref[...] = image_grad[i * block : (i + 1) * block].astype(ref.dtype)


def pair_terms(first, scalars, chunks, packets):
    block, width = chunks[0].shape
    count, wide = packets[0].shape
    rows, texts = len(chunks) * block, 2 * count
    anywhere = pl.BlockSpec(memory_space=pl.ANY)
    return pl.pallas_call(
        lambda *refs: pair_kernel(len(chunks), *refs),
        in_specs=[smem, smem] + [anywhere] * (len(chunks) + 2),
        out_specs=[vmem] * (len(chunks) + 2),
        out_shape=[jax.ShapeDtypeStruct((count, width), jnp.bfloat16)] * 2
        + [jax.ShapeDtypeStruct((block, width), jnp.bfloat16)] * len(chunks),
        scratch_shapes=[
            pltpu.VMEM((rows, width), jnp.bfloat16),
            pltpu.VMEM((texts, wide), jnp.bfloat16),
            pltpu.SemaphoreType.DMA((len(chunks) + 2,)),
        ],
        compiler_params=params(),
        cost_estimate=pl.CostEstimate(
            flops=6 * rows * texts * width, bytes_accessed=4 * (rows + texts) * width, transcendentals=2 * rows * texts
        ),
    )(first, scalars, *chunks, *packets)


def backward_kernel(embed_ref, *refs):
    floats = embed_ref[...].astype(jnp.float32)
    inverse = inverse_norm(floats)
    unit = floats * inverse
    parts_refs, out_ref = refs[:-1], refs[-1]
    grad = None
    for ref in parts_refs:
        parts = [ref[i] for i in range(ref.shape[0])] if len(ref.shape) == 3 else [ref[...]]
        for part in parts:
            part = part.astype(jnp.float32)
            grad = part if grad is None else grad + part
    along = jnp.sum(unit * grad, axis=-1, keepdims=True)
    out_ref[...] = ((grad - unit * along) * inverse).astype(out_ref.dtype)


def unit_backward(embed, *parts):
    return pl.pallas_call(
        backward_kernel,
        in_specs=[vmem] * (1 + len(parts)),
        out_specs=vmem,
        out_shape=jax.ShapeDtypeStruct(embed.shape, jnp.bfloat16),
        compiler_params=params(),
    )(embed, *parts)


def spread(copies, axis):
    return lax.all_to_all(copies, axis, split_axis=0, concat_axis=0, tiled=True).reshape(-1, copies.shape[2])


def parted(rows, axis):
    parts = rows.reshape(lax.axis_size(axis), -1, rows.shape[1])
    return lax.all_to_all(parts, axis, split_axis=0, concat_axis=0, tiled=True)


def on_device(image_embed, text_embed, log_scale, logit_bias, pair_index):
    own_images = image_embed.shape[0]
    ring = lax.axis_size("x")
    together = lax.optimization_barrier

    unit, packets = units_and_packets(pair_index, image_embed, text_embed, lax.axis_size("z"))
    texts, beside = together((spread(packets, "z"), shifted(unit, "yl", 1)))
    pair = jnp.concatenate([unit, beside], axis=0)
    copies = jnp.broadcast_to(texts[None], (lax.axis_size(MIDDLE),) + texts.shape)
    copies, pair = together((copies, pair))
    own, *chunks = together((spread(copies, MIDDLE), *[shifted(pair, "x", s) for s in range(1, ring)]))
    other = shifted(own, "c", 1)

    scale = jnp.exp(log_scale)
    scalars = jnp.concatenate([scale, -math.log2(math.e) * scale, -math.log2(math.e) * logit_bias])
    far, yl, x, c = lax.axis_index(FAR), lax.axis_index("yl"), lax.axis_index("x"), lax.axis_index("c")
    first = jnp.stack(
        [
            (((far * 2 + place) * ring + (x - s) % ring) * 2 + c) * own_images
            for s in range(ring)
            for place in (yl, 1 - yl)
        ]
    ).astype(jnp.int32)
    own_part, other_part, *image_parts = pair_terms(first, scalars, [pair] + chunks, [own, other])

    text_part = own_part.astype(jnp.float32) + shifted(other_part, "c", 1).astype(jnp.float32)
    text_parts, *returned = together(
        (parted(text_part.astype(jnp.bfloat16), MIDDLE), *[shifted(image_parts[s], "x", -s) for s in range(1, ring)])
    )
    text_part = jnp.sum(text_parts.astype(jnp.float32), axis=0).astype(jnp.bfloat16)
    image_total = image_parts[0].astype(jnp.float32) + sum(part.astype(jnp.float32) for part in returned)
    image_own, image_beside = image_total[:own_images], image_total[own_images:].astype(jnp.bfloat16)
    text_part, image_beside = together((text_part, image_beside))
    text_parts, beside = together((parted(text_part, "z"), shifted(image_beside, "yl", 1)))
    return (
        unit_backward(image_embed, image_own, beside),
        unit_backward(text_embed, text_parts),
    )


def solution(mesh):
    split = Mesh(mesh.devices.reshape(SIZES), AXES)
    rows = P(AXES, None)
    return jax.shard_map(
        on_device,
        mesh=split,
        in_specs=(rows, rows, P(), P(), P(AXES)),
        out_specs=(rows, rows),
        check_vma=False,
    )
```

```python
import math

import jax
import jax.numpy as jnp
from jax import lax
from jax.experimental import pallas as pl
from jax.experimental.pallas import tpu as pltpu
from jax.sharding import Mesh
from jax.sharding import PartitionSpec as P

AXES = ("z", "yh", "ym", "yl", "x", "c")
SIZES = (8, 2, 2, 2, 4, 2)
FAR = ("z", "yh", "ym")
LANES = 128
VMEM = 40 * 1024 * 1024
ROWS_BY_ROWS = (((1,), (1,)), ((), ()))
COLUMNS_BY_ROWS = (((0,), (0,)), ((), ()))

smem = pl.BlockSpec(memory_space=pltpu.SMEM)
vmem = pl.BlockSpec(memory_space=pltpu.VMEM)


def params():
    return pltpu.CompilerParams(vmem_limit_bytes=VMEM)


def shifted(array, axis, by):
    devices = lax.axis_size(axis)
    return lax.ppermute(array, axis, [(i, (i + by) % devices) for i in range(devices)])


def inverse_norm(floats):
    return lax.rsqrt(jnp.sum(floats * floats, axis=-1, keepdims=True) + 1e-06)


def unit_kernel(pair_ref, image_ref, text_ref, unit_ref, packet_ref):
    floats = image_ref[...].astype(jnp.float32)
    unit_ref[...] = (floats * inverse_norm(floats)).astype(unit_ref.dtype)
    rows, width = text_ref.shape
    floats = text_ref[...].astype(jnp.float32)
    unit = (floats * inverse_norm(floats)).astype(packet_ref.dtype)
    row = lax.broadcasted_iota(jnp.int32, (rows, LANES), 0)
    lane = lax.broadcasted_iota(jnp.int32, (rows, LANES), 1)
    index = jnp.zeros((rows, LANES), jnp.int32)
    for i in range(rows):
        index = jnp.where(row == i, pair_ref[i], index)
    digits = jnp.where(lane == 0, index >> 8, jnp.where(lane == 1, index & 255, 0))
    digits = digits.astype(jnp.float32).astype(packet_ref.dtype)
    for peer in range(packet_ref.shape[0]):
        packet_ref[peer, :, :width] = unit
        packet_ref[peer, :, width:] = digits


def units_and_packets(pair_index, image_embed, text_embed, peers):
    rows, width = text_embed.shape
    return pl.pallas_call(
        unit_kernel,
        in_specs=[smem, vmem, vmem],
        out_specs=[vmem, vmem],
        out_shape=[
            jax.ShapeDtypeStruct(image_embed.shape, jnp.bfloat16),
            jax.ShapeDtypeStruct((peers, rows, width + LANES), jnp.bfloat16),
        ],
        compiler_params=params(),
    )(pair_index, image_embed, text_embed)


def pair_kernel(chunks, first_ref, scalars_ref, *refs):
    chunk_refs, packet_refs = refs[:chunks], refs[chunks : chunks + 2]
    text_grad_refs = refs[chunks + 2 : chunks + 4]
    image_grad_refs = refs[chunks + 4 : -2]
    image_ref, text_ref = refs[-2:]
    block, width = chunk_refs[0].shape
    count = packet_refs[0].shape[0]
    for i, ref in enumerate(chunk_refs):
        image_ref[i * block : (i + 1) * block, :] = ref[...]
    for i, ref in enumerate(packet_refs):
        text_ref[i * count : (i + 1) * count, :] = ref[...]

    digits = text_ref[:, width:].astype(jnp.float32).T
    pairs = (digits[0:1] * 256.0 + digits[1:2]).astype(jnp.int32)
    row = lax.broadcasted_iota(jnp.int32, (128, 1), 0)
    rows = jnp.concatenate([row + first_ref[p] for p in range(chunks * block // 128)], axis=0)
    images = image_ref[...]
    texts = text_ref[:, :width]
    dots = lax.dot_general(images, texts, ROWS_BY_ROWS, preferred_element_type=jnp.float32)
    chance = 1.0 / (1.0 + jnp.exp2(dots * scalars_ref[1] + scalars_ref[2]))
    weight = (scalars_ref[0] * jnp.where(pairs == rows, chance - 1.0, chance)).astype(jnp.bfloat16)
    text_grad = lax.dot_general(weight, images, COLUMNS_BY_ROWS, preferred_element_type=jnp.float32)
    for i, ref in enumerate(text_grad_refs):
        ref[...] = text_grad[i * count : (i + 1) * count].astype(ref.dtype)
    image_grad = jnp.dot(weight, texts, preferred_element_type=jnp.float32)
    for i, ref in enumerate(image_grad_refs):
        ref[...] = image_grad[i * ref.shape[0] : (i + 1) * ref.shape[0]].astype(ref.dtype)


def pair_terms(first, scalars, chunks, packets, shares):
    block, width = chunks[0].shape
    count, wide = packets[0].shape
    rows, texts = len(chunks) * block, 2 * count
    return pl.pallas_call(
        lambda *refs: pair_kernel(len(chunks), *refs),
        in_specs=[smem, smem] + [vmem] * (len(chunks) + 2),
        out_specs=[vmem] * (shares + 2),
        out_shape=[jax.ShapeDtypeStruct((count, width), jnp.bfloat16)] * 2
        + [jax.ShapeDtypeStruct((rows // shares, width), jnp.bfloat16)] * shares,
        scratch_shapes=[
            pltpu.VMEM((rows, width), jnp.bfloat16),
            pltpu.VMEM((texts, wide), jnp.bfloat16),
        ],
        compiler_params=params(),
        cost_estimate=pl.CostEstimate(
            flops=6 * rows * texts * width, bytes_accessed=4 * (rows + texts) * width, transcendentals=2 * rows * texts
        ),
    )(first, scalars, *chunks, *packets)


def backward_kernel(embed_ref, *refs):
    floats = embed_ref[...].astype(jnp.float32)
    inverse = inverse_norm(floats)
    unit = floats * inverse
    parts_refs, out_ref = refs[:-1], refs[-1]
    grad = None
    for ref in parts_refs:
        parts = [ref[i] for i in range(ref.shape[0])] if len(ref.shape) == 3 else [ref[...]]
        for part in parts:
            part = part.astype(jnp.float32)
            grad = part if grad is None else grad + part
    along = jnp.sum(unit * grad, axis=-1, keepdims=True)
    out_ref[...] = ((grad - unit * along) * inverse).astype(out_ref.dtype)


def unit_backward(embed, *parts):
    return pl.pallas_call(
        backward_kernel,
        in_specs=[vmem] * (1 + len(parts)),
        out_specs=vmem,
        out_shape=jax.ShapeDtypeStruct(embed.shape, jnp.bfloat16),
        compiler_params=params(),
    )(embed, *parts)


def spread(copies, axis):
    return lax.all_to_all(copies, axis, split_axis=0, concat_axis=0, tiled=True).reshape(-1, copies.shape[2])


def parted(rows, axis):
    parts = rows.reshape(lax.axis_size(axis), -1, rows.shape[1])
    return lax.all_to_all(parts, axis, split_axis=0, concat_axis=0, tiled=True)


def gathered(rows, by, across):
    pairs, ring = lax.axis_size("yl"), lax.axis_size("x")
    moves = [
        (p * ring + i, (p + across) % pairs * ring + (i + by) % ring) for p in range(pairs) for i in range(ring)
    ]
    return lax.ppermute(rows, ("yl", "x"), moves)


def on_device(image_embed, text_embed, log_scale, logit_bias, pair_index):
    own_images = image_embed.shape[0]
    ring = lax.axis_size("x")
    together = lax.optimization_barrier

    unit, packets = units_and_packets(pair_index, image_embed, text_embed, lax.axis_size(FAR))
    places = [(s, p) for s in range(ring) for p in range(2)]
    own, *chunks = together((spread(packets, FAR), *[gathered(unit, s, p) for s, p in places[1:]]))
    other = shifted(own, "c", 1)

    scale = jnp.exp(log_scale)
    scalars = jnp.concatenate([scale, -math.log2(math.e) * scale, -math.log2(math.e) * logit_bias])
    far, yl, x, c = lax.axis_index(FAR), lax.axis_index("yl"), lax.axis_index("x"), lax.axis_index("c")
    first = jnp.stack(
        [
            (((far * 2 + place) * ring + (x - s) % ring) * 2 + c) * own_images
            for s in range(ring)
            for place in (yl, 1 - yl)
        ]
    ).astype(jnp.int32)
    own_part, other_part, *image_parts = pair_terms(
        first, scalars, [unit] + chunks, [own, other], ring
    )

    text_part = own_part.astype(jnp.float32) + shifted(other_part, "c", 1).astype(jnp.float32)
    text_parts = parted(text_part.astype(jnp.bfloat16), FAR)
    returned = [shifted(image_parts[s], "x", -s) for s in range(1, ring)]
    image_total = image_parts[0].astype(jnp.float32) + sum(part.astype(jnp.float32) for part in returned)
    image_own, image_beside = image_total[:own_images], image_total[own_images:].astype(jnp.bfloat16)
    beside = shifted(image_beside, "yl", 1)
    return (
        unit_backward(image_embed, image_own, beside),
        unit_backward(text_embed, text_parts),
    )


def solution(mesh):
    split = Mesh(mesh.devices.reshape(SIZES), AXES)
    rows = P(AXES, None)
    return jax.shard_map(
        on_device,
        mesh=split,
        in_specs=(rows, rows, P(), P(), P(AXES)),
        out_specs=(rows, rows),
        check_vma=False,
    )
```

```python
import math

import jax
import jax.numpy as jnp
from jax import lax
from jax.experimental import pallas as pl
from jax.experimental.pallas import tpu as pltpu
from jax.sharding import Mesh
from jax.sharding import PartitionSpec as P

AXES = ("z", "y", "x", "c")
SIZES = (8, 8, 4, 2)
LANES = 128
MIB = 1024 * 1024
ROWS_BY_ROWS = (((1,), (1,)), ((), ()))
COLUMNS_BY_ROWS = (((0,), (0,)), ((), ()))

smem = pl.BlockSpec(memory_space=pltpu.SMEM)
vmem = pl.BlockSpec(memory_space=pltpu.VMEM)


def params(mib):
    return pltpu.CompilerParams(vmem_limit_bytes=mib * MIB)


def inverse_norm(floats):
    return lax.rsqrt(jnp.sum(floats * floats, axis=-1, keepdims=True) + 1e-06)


def unit_kernel(embed_ref, unit_ref):
    floats = embed_ref[...].astype(jnp.float32)
    unit_ref[...] = (floats * inverse_norm(floats)).astype(unit_ref.dtype)


def units(embed):
    return pl.pallas_call(
        unit_kernel,
        in_specs=[vmem],
        out_specs=vmem,
        out_shape=jax.ShapeDtypeStruct(embed.shape, jnp.bfloat16),
        compiler_params=params(56),
    )(embed)


def packet_kernel(pair_ref, text_ref, packet_ref):
    rows, width = text_ref.shape
    floats = text_ref[...].astype(jnp.float32)
    unit = (floats * inverse_norm(floats)).astype(packet_ref.dtype)
    row = lax.broadcasted_iota(jnp.int32, (rows, LANES), 0)
    lane = lax.broadcasted_iota(jnp.int32, (rows, LANES), 1)
    index = jnp.zeros((rows, LANES), jnp.int32)
    for i in range(rows):
        index = jnp.where(row == i, pair_ref[i], index)
    digits = jnp.where(lane == 0, index >> 8, jnp.where(lane == 1, index & 255, 0))
    digits = digits.astype(jnp.float32).astype(packet_ref.dtype)
    for peer in range(packet_ref.shape[0]):
        packet_ref[peer, :, :width] = unit
        packet_ref[peer, :, width:] = digits


def text_packets(pair_index, embed, peers):
    rows, width = embed.shape
    return pl.pallas_call(
        packet_kernel,
        in_specs=[smem, vmem],
        out_specs=vmem,
        out_shape=jax.ShapeDtypeStruct((peers, rows, width + LANES), jnp.bfloat16),
        compiler_params=params(56),
    )(pair_index, embed)


def pair_kernel(first_ref, scalars_ref, images_ref, own_ref, other_ref, *refs):
    image_grad_ref, own_grad_ref, other_grad_ref, image_ref, text_ref, sem = refs
    copy = pltpu.make_async_copy(images_ref, image_ref, sem)
    copy.start()
    width = image_ref.shape[1]
    count = own_ref.shape[0]
    text_ref[:count, :] = own_ref[...]
    text_ref[count:, :] = other_ref[...]
    digits = text_ref[:, width:].astype(jnp.float32).T
    pairs = (digits[0:1] * 256.0 + digits[1:2]).astype(jnp.int32)
    row = lax.broadcasted_iota(jnp.int32, (128, 1), 0)
    rows = jnp.concatenate([row + first_ref[p] for p in range(image_ref.shape[0] // 128)], axis=0)
    texts = text_ref[:, :width]
    copy.wait()
    images = image_ref[...]
    dots = lax.dot_general(images, texts, ROWS_BY_ROWS, preferred_element_type=jnp.float32)
    chance = 1.0 / (1.0 + jnp.exp2(dots * scalars_ref[1] + scalars_ref[2]))
    weight = (scalars_ref[0] * jnp.where(pairs == rows, chance - 1.0, chance)).astype(jnp.bfloat16)
    image_grad_ref[...] = jnp.dot(weight, texts, preferred_element_type=jnp.float32).astype(image_grad_ref.dtype)
    text_grad = lax.dot_general(weight, images, COLUMNS_BY_ROWS, preferred_element_type=jnp.float32)
    own_grad_ref[...] = text_grad[:count].astype(own_grad_ref.dtype)
    other_grad_ref[...] = text_grad[count:].astype(other_grad_ref.dtype)


def pair_terms(first, scalars, images, own, other):
    rows, width = images.shape
    count, wide = own.shape
    texts = 2 * count
    return pl.pallas_call(
        pair_kernel,
        in_specs=[smem, smem, pl.BlockSpec(memory_space=pl.ANY), vmem, vmem],
        out_specs=[vmem] * 3,
        out_shape=[
            jax.ShapeDtypeStruct((rows, width), jnp.bfloat16),
            jax.ShapeDtypeStruct((count, width), jnp.bfloat16),
            jax.ShapeDtypeStruct((count, width), jnp.bfloat16),
        ],
        scratch_shapes=[
            pltpu.VMEM((rows, width), jnp.bfloat16),
            pltpu.VMEM((texts, wide), jnp.bfloat16),
            pltpu.SemaphoreType.DMA,
        ],
        compiler_params=params(32),
        cost_estimate=pl.CostEstimate(
            flops=6 * rows * texts * width, bytes_accessed=4 * (rows + texts) * width, transcendentals=2 * rows * texts
        ),
    )(first, scalars, images, own, other)


def project(embed_ref, grad, out_ref):
    floats = embed_ref[...].astype(jnp.float32)
    inverse = inverse_norm(floats)
    unit = floats * inverse
    along = jnp.sum(unit * grad, axis=-1, keepdims=True)
    out_ref[...] = ((grad - unit * along) * inverse).astype(out_ref.dtype)


def backward_kernel(image_ref, text_ref, image_grad_ref, text_grads_ref, image_out_ref, text_out_ref):
    project(image_ref, image_grad_ref[...].astype(jnp.float32), image_out_ref)
    text_grad = text_grads_ref[0].astype(jnp.float32)
    for part in range(1, text_grads_ref.shape[0]):
        text_grad += text_grads_ref[part].astype(jnp.float32)
    project(text_ref, text_grad, text_out_ref)


def unit_backward(image_embed, text_embed, image_grad, text_grads):
    return pl.pallas_call(
        backward_kernel,
        in_specs=[vmem] * 4,
        out_specs=[vmem] * 2,
        out_shape=[
            jax.ShapeDtypeStruct(image_embed.shape, jnp.bfloat16),
            jax.ShapeDtypeStruct(text_embed.shape, jnp.bfloat16),
        ],
        compiler_params=params(8),
    )(image_embed, text_embed, image_grad, text_grads)


def image_rings():
    depth, length, width, cores = SIZES
    rings = []
    for z in range(depth):
        for x in range(width):
            for c in range(cores):
                ring = [((z * length + y) * width + x) * cores + c for y in range(length)]
                rings.append(ring if c == 0 else ring[::-1])
    return rings


def exchanged(array):
    return lax.ppermute(array, "c", [(0, 1), (1, 0)])


def spread(copies, axis):
    return lax.all_to_all(copies, axis, split_axis=0, concat_axis=0, tiled=True).reshape(-1, copies.shape[2])


def parted(rows, axis):
    parts = rows.reshape(lax.axis_size(axis), -1, rows.shape[1])
    return lax.all_to_all(parts, axis, split_axis=0, concat_axis=0, tiled=True)


def on_device(image_embed, text_embed, log_scale, logit_bias, pair_index):
    own_images = image_embed.shape[0]
    rings = image_rings()
    images = lax.all_gather(units(image_embed), AXES, axis=0, tiled=True, axis_index_groups=rings)

    texts = spread(text_packets(pair_index, text_embed, lax.axis_size("z")), "z")
    own = spread(jnp.broadcast_to(texts[None], (lax.axis_size("x"),) + texts.shape), "x")
    other = exchanged(own)

    scale = jnp.exp(log_scale)
    scalars = jnp.concatenate([scale, -math.log2(math.e) * scale, -math.log2(math.e) * logit_bias])
    z, x, c = lax.axis_index("z"), lax.axis_index("x"), lax.axis_index("c")
    place = jnp.arange(SIZES[1], dtype=jnp.int32)
    place = jnp.where(c == 0, place, SIZES[1] - 1 - place)
    first = (((z * SIZES[1] + place) * SIZES[2] + x) * SIZES[3] + c) * own_images

    image_part, own_part, other_part = pair_terms(first.astype(jnp.int32), scalars, images, own, other)
    image_grad = lax.psum_scatter(image_part, AXES, scatter_dimension=0, tiled=True, axis_index_groups=rings)

    text_part = own_part.astype(jnp.float32) + exchanged(other_part).astype(jnp.float32)
    text_part = jnp.sum(parted(text_part.astype(jnp.bfloat16), "x").astype(jnp.float32), axis=0)
    text_grads = parted(text_part.astype(jnp.bfloat16), "z")
    return unit_backward(image_embed, text_embed, image_grad, text_grads)


def solution(mesh):
    split = Mesh(mesh.devices.reshape(SIZES), AXES)
    rows = P(AXES, None)
    return jax.shard_map(
        on_device,
        mesh=split,
        in_specs=(rows, rows, P(), P(), P(AXES)),
        out_specs=(rows, rows),
        check_vma=False,
    )
```

```python
import math

import jax
import jax.numpy as jnp
from jax import lax
from jax.experimental import pallas as pl
from jax.experimental.pallas import tpu as pltpu
from jax.sharding import Mesh
from jax.sharding import PartitionSpec as P

AXES = ("z", "yh", "ym", "yl", "x", "c")
SIZES = (8, 2, 2, 2, 4, 2)
MIDDLE = ("yh", "ym")
LANES = 128
MIB = 1024 * 1024
ROWS_BY_ROWS = (((1,), (1,)), ((), ()))
COLUMNS_BY_ROWS = (((0,), (0,)), ((), ()))

smem = pl.BlockSpec(memory_space=pltpu.SMEM)
vmem = pl.BlockSpec(memory_space=pltpu.VMEM)


def params(mib):
    return pltpu.CompilerParams(vmem_limit_bytes=mib * MIB)


def inverse_norm(floats):
    return lax.rsqrt(jnp.sum(floats * floats, axis=-1, keepdims=True) + 1e-06)


def unit_kernel(pair_ref, image_ref, text_ref, unit_ref, packet_ref):
    floats = image_ref[...].astype(jnp.float32)
    unit_ref[...] = (floats * inverse_norm(floats)).astype(unit_ref.dtype)
    rows, width = text_ref.shape
    floats = text_ref[...].astype(jnp.float32)
    unit = (floats * inverse_norm(floats)).astype(packet_ref.dtype)
    row = lax.broadcasted_iota(jnp.int32, (rows, LANES), 0)
    lane = lax.broadcasted_iota(jnp.int32, (rows, LANES), 1)
    index = jnp.zeros((rows, LANES), jnp.int32)
    for i in range(rows):
        index = jnp.where(row == i, pair_ref[i], index)
    digits = jnp.where(lane == 0, index >> 8, jnp.where(lane == 1, index & 255, 0))
    digits = digits.astype(jnp.float32).astype(packet_ref.dtype)
    for peer in range(packet_ref.shape[0]):
        packet_ref[peer, :, :width] = unit
        packet_ref[peer, :, width:] = digits


def units_and_packets(pair_index, image_embed, text_embed, peers):
    rows, width = text_embed.shape
    return pl.pallas_call(
        unit_kernel,
        in_specs=[smem, vmem, vmem],
        out_specs=[vmem, vmem],
        out_shape=[
            jax.ShapeDtypeStruct(image_embed.shape, jnp.bfloat16),
            jax.ShapeDtypeStruct((peers, rows, width + LANES), jnp.bfloat16),
        ],
        compiler_params=params(56),
    )(pair_index, image_embed, text_embed)


def pair_kernel(chunks, first_ref, scalars_ref, image_ref, *refs):
    chunk_refs, other_ref = refs[:chunks], refs[chunks]
    image_grad_ref, other_grad_ref, text_ref = refs[chunks + 1], refs[chunks + 2], refs[-1]
    own_grad_refs = refs[chunks + 3 : -1]
    rows, width = image_ref.shape
    size = chunk_refs[0].shape[0]
    count = chunks * size
    for i, ref in enumerate(chunk_refs):
        text_ref[i * size : (i + 1) * size, :] = ref[...]
    text_ref[count:, :] = other_ref[...]
    digits = text_ref[:, width:].astype(jnp.float32).T
    pairs = (digits[0:1] * 256.0 + digits[1:2]).astype(jnp.int32)
    row = lax.broadcasted_iota(jnp.int32, (128, 1), 0)
    places = jnp.concatenate([row + first_ref[p] for p in range(rows // 128)], axis=0)
    images = image_ref[...]
    texts = text_ref[:, :width]
    dots = lax.dot_general(images, texts, ROWS_BY_ROWS, preferred_element_type=jnp.float32)
    chance = 1.0 / (1.0 + jnp.exp2(dots * scalars_ref[1] + scalars_ref[2]))
    weight = (scalars_ref[0] * jnp.where(pairs == places, chance - 1.0, chance)).astype(jnp.bfloat16)
    image_grad_ref[...] = jnp.dot(weight, texts, preferred_element_type=jnp.float32).astype(image_grad_ref.dtype)
    text_grad = lax.dot_general(weight, images, COLUMNS_BY_ROWS, preferred_element_type=jnp.float32)
    for i, ref in enumerate(own_grad_refs):
        ref[...] = text_grad[i * size : (i + 1) * size].astype(ref.dtype)
    other_grad_ref[...] = text_grad[count:].astype(other_grad_ref.dtype)


def pair_terms(first, scalars, images, chunks, other):
    rows, width = images.shape
    size, wide = chunks[0].shape
    count = other.shape[0]
    texts = 2 * count
    return pl.pallas_call(
        lambda *refs: pair_kernel(len(chunks), *refs),
        in_specs=[smem, smem] + [vmem] * (len(chunks) + 2),
        out_specs=[vmem] * (len(chunks) + 2),
        out_shape=[
            jax.ShapeDtypeStruct((rows, width), jnp.bfloat16),
            jax.ShapeDtypeStruct((count, width), jnp.bfloat16),
        ]
        + [jax.ShapeDtypeStruct((size, width), jnp.bfloat16)] * len(chunks),
        scratch_shapes=[pltpu.VMEM((texts, wide), jnp.bfloat16)],
        compiler_params=params(32),
        cost_estimate=pl.CostEstimate(
            flops=6 * rows * texts * width, bytes_accessed=4 * (rows + texts) * width, transcendentals=2 * rows * texts
        ),
    )(first, scalars, images, *chunks, other)


def project(embed_ref, grad, out_ref):
    floats = embed_ref[...].astype(jnp.float32)
    inverse = inverse_norm(floats)
    unit = floats * inverse
    along = jnp.sum(unit * grad, axis=-1, keepdims=True)
    out_ref[...] = ((grad - unit * along) * inverse).astype(out_ref.dtype)


def backward_kernel(image_ref, text_ref, image_grad_ref, beside_ref, text_grads_ref, image_out_ref, text_out_ref):
    project(image_ref, image_grad_ref[...] + beside_ref[...].astype(jnp.float32), image_out_ref)
    text_grad = text_grads_ref[0].astype(jnp.float32)
    for part in range(1, text_grads_ref.shape[0]):
        text_grad += text_grads_ref[part].astype(jnp.float32)
    project(text_ref, text_grad, text_out_ref)


def unit_backward(image_embed, text_embed, image_grad, beside, text_grads):
    return pl.pallas_call(
        backward_kernel,
        in_specs=[vmem] * 5,
        out_specs=[vmem] * 2,
        out_shape=[
            jax.ShapeDtypeStruct(image_embed.shape, jnp.bfloat16),
            jax.ShapeDtypeStruct(text_embed.shape, jnp.bfloat16),
        ],
        compiler_params=params(8),
    )(image_embed, text_embed, image_grad, beside, text_grads)


def shifted(array, axis, by):
    devices = lax.axis_size(axis)
    return lax.ppermute(array, axis, [(i, (i + by) % devices) for i in range(devices)])


def spread(copies, axis):
    return lax.all_to_all(copies, axis, split_axis=0, concat_axis=0, tiled=True).reshape(-1, copies.shape[2])


def parted(rows, axis):
    parts = rows.reshape(lax.axis_size(axis), -1, rows.shape[1])
    return lax.all_to_all(parts, axis, split_axis=0, concat_axis=0, tiled=True)


def total(parts):
    return sum(part.astype(jnp.float32) for part in parts)


def on_device(image_embed, text_embed, log_scale, logit_bias, pair_index):
    own_images = image_embed.shape[0]
    own_texts = text_embed.shape[0] * lax.axis_size("z")
    ring, middle = lax.axis_size("x"), lax.axis_size(MIDDLE)
    together = lax.optimization_barrier

    unit, packets = units_and_packets(pair_index, image_embed, text_embed, lax.axis_size("z"))
    texts, beside = together((spread(packets, "z"), shifted(unit, "yl", 1)))
    pair = jnp.concatenate([unit, beside], axis=0)
    copies = jnp.broadcast_to(pair[None], (ring,) + pair.shape)
    images, *chunks = together((spread(copies, "x"), *[shifted(texts, MIDDLE, s) for s in range(1, middle)]))
    chunks = [texts] + chunks
    other = shifted(jnp.concatenate(chunks, axis=0), "c", 1)

    scale = jnp.exp(log_scale)
    scalars = jnp.concatenate([scale, -math.log2(math.e) * scale, -math.log2(math.e) * logit_bias])
    far, yl, c = lax.axis_index(("z",) + MIDDLE), lax.axis_index("yl"), lax.axis_index("c")
    first = jnp.stack(
        [(((far * 2 + place) * ring + x) * 2 + c) * own_images for x in range(ring) for place in (yl, 1 - yl)]
    ).astype(jnp.int32)
    image_part, other_part, *own_parts = pair_terms(first, scalars, images, chunks, other)

    back = shifted(other_part, "c", 1)
    sums = [
        total([part, back[s * own_texts : (s + 1) * own_texts]]).astype(jnp.bfloat16) for s, part in enumerate(own_parts)
    ]
    image_parts, *returned = together(
        (parted(image_part, "x"), *[shifted(sums[s], MIDDLE, -s) for s in range(1, middle)])
    )
    text_part = total([sums[0]] + returned).astype(jnp.bfloat16)
    image_total = jnp.sum(image_parts.astype(jnp.float32), axis=0)
    image_own, image_beside = image_total[:own_images], image_total[own_images:].astype(jnp.bfloat16)
    text_part, image_beside = together((text_part, image_beside))
    text_grads, beside = together((parted(text_part, "z"), shifted(image_beside, "yl", 1)))
    return unit_backward(image_embed, text_embed, image_own, beside, text_grads)


def solution(mesh):
    split = Mesh(mesh.devices.reshape(SIZES), AXES)
    rows = P(AXES, None)
    return jax.shard_map(
        on_device,
        mesh=split,
        in_specs=(rows, rows, P(), P(), P(AXES)),
        out_specs=(rows, rows),
        check_vma=False,
    )
```

```python
import math

import jax
import jax.numpy as jnp
from jax import lax
from jax.experimental import pallas as pl
from jax.experimental.pallas import tpu as pltpu
from jax.sharding import Mesh
from jax.sharding import PartitionSpec as P

AXES = ("z", "y", "x", "c")
SIZES = (8, 8, 4, 2)
LANES = 128
MIB = 1024 * 1024
ROWS_BY_ROWS = (((1,), (1,)), ((), ()))
COLUMNS_BY_ROWS = (((0,), (0,)), ((), ()))

smem = pl.BlockSpec(memory_space=pltpu.SMEM)
vmem = pl.BlockSpec(memory_space=pltpu.VMEM)


def params(mib):
    return pltpu.CompilerParams(vmem_limit_bytes=mib * MIB)


def inverse_norm(floats):
    return lax.rsqrt(jnp.sum(floats * floats, axis=-1, keepdims=True) + 1e-06)


def packet_kernel(pair_ref, text_ref, packet_ref):
    rows, width = text_ref.shape
    floats = text_ref[...].astype(jnp.float32)
    unit = (floats * inverse_norm(floats)).astype(packet_ref.dtype)
    row = lax.broadcasted_iota(jnp.int32, (rows, LANES), 0)
    lane = lax.broadcasted_iota(jnp.int32, (rows, LANES), 1)
    index = jnp.zeros((rows, LANES), jnp.int32)
    for i in range(rows):
        index = jnp.where(row == i, pair_ref[i], index)
    digits = jnp.where(lane == 0, index >> 8, jnp.where(lane == 1, index & 255, 0))
    digits = digits.astype(jnp.float32).astype(packet_ref.dtype)
    for peer in range(packet_ref.shape[0]):
        packet_ref[peer, :, :width] = unit
        packet_ref[peer, :, width:] = digits


def text_packets(pair_index, embed, peers):
    rows, width = embed.shape
    return pl.pallas_call(
        packet_kernel,
        in_specs=[smem, vmem],
        out_specs=vmem,
        out_shape=jax.ShapeDtypeStruct((peers, rows, width + LANES), jnp.bfloat16),
        compiler_params=params(56),
    )(pair_index, embed)


def weight_kernel(first_ref, scalars_ref, image_ref, own_ref, other_ref, *refs):
    image_grad_ref, weight_ref, unit_ref, text_ref = refs
    width = image_ref.shape[1]
    count = own_ref.shape[0]
    text_ref[:count, :] = own_ref[...]
    text_ref[count:, :] = other_ref[...]
    digits = text_ref[:, width:].astype(jnp.float32).T
    pairs = (digits[0:1] * 256.0 + digits[1:2]).astype(jnp.int32)
    row = lax.broadcasted_iota(jnp.int32, (128, 1), 0)
    rows = jnp.concatenate([row + first_ref[p] for p in range(image_ref.shape[0] // 128)], axis=0)
    texts = text_ref[:, :width]
    floats = image_ref[...].astype(jnp.float32)
    images = (floats * inverse_norm(floats)).astype(unit_ref.dtype)
    unit_ref[...] = images
    dots = lax.dot_general(images, texts, ROWS_BY_ROWS, preferred_element_type=jnp.float32)
    chance = 1.0 / (1.0 + jnp.exp2(dots * scalars_ref[1] + scalars_ref[2]))
    weight = (scalars_ref[0] * jnp.where(pairs == rows, chance - 1.0, chance)).astype(jnp.bfloat16)
    weight_ref[...] = weight
    image_grad_ref[...] = jnp.dot(weight, texts, preferred_element_type=jnp.float32).astype(image_grad_ref.dtype)


def weights_and_image_terms(first, scalars, images, own, other):
    rows, width = images.shape
    count, wide = own.shape
    texts = 2 * count
    return pl.pallas_call(
        weight_kernel,
        in_specs=[smem, smem, vmem, vmem, vmem],
        out_specs=[vmem] * 3,
        out_shape=[
            jax.ShapeDtypeStruct((rows, width), jnp.bfloat16),
            jax.ShapeDtypeStruct((rows, texts), jnp.bfloat16),
            jax.ShapeDtypeStruct((rows, width), jnp.bfloat16),
        ],
        scratch_shapes=[pltpu.VMEM((texts, wide), jnp.bfloat16)],
        compiler_params=params(32),
        cost_estimate=pl.CostEstimate(
            flops=4 * rows * texts * width, bytes_accessed=4 * (rows + texts) * width, transcendentals=2 * rows * texts
        ),
    )(first, scalars, images, own, other)


def text_kernel(weight_ref, unit_ref, own_grad_ref, other_grad_ref):
    count = own_grad_ref.shape[0]
    grad = lax.dot_general(weight_ref[...], unit_ref[...], COLUMNS_BY_ROWS, preferred_element_type=jnp.float32)
    own_grad_ref[...] = grad[:count].astype(own_grad_ref.dtype)
    other_grad_ref[...] = grad[count:].astype(other_grad_ref.dtype)


def text_terms(weights, units):
    rows, texts = weights.shape
    width = units.shape[1]
    return pl.pallas_call(
        text_kernel,
        in_specs=[vmem] * 2,
        out_specs=[vmem] * 2,
        out_shape=[jax.ShapeDtypeStruct((texts // 2, width), jnp.bfloat16)] * 2,
        compiler_params=params(24),
        cost_estimate=pl.CostEstimate(
            flops=2 * rows * texts * width, bytes_accessed=2 * (rows + texts) * width, transcendentals=0
        ),
    )(weights, units)


def project(embed_ref, grad, out_ref):
    floats = embed_ref[...].astype(jnp.float32)
    inverse = inverse_norm(floats)
    unit = floats * inverse
    along = jnp.sum(unit * grad, axis=-1, keepdims=True)
    out_ref[...] = ((grad - unit * along) * inverse).astype(out_ref.dtype)


def backward_kernel(image_ref, text_ref, image_grad_ref, text_grads_ref, image_out_ref, text_out_ref):
    project(image_ref, image_grad_ref[...].astype(jnp.float32), image_out_ref)
    text_grad = text_grads_ref[0].astype(jnp.float32)
    for part in range(1, text_grads_ref.shape[0]):
        text_grad += text_grads_ref[part].astype(jnp.float32)
    project(text_ref, text_grad, text_out_ref)


def unit_backward(image_embed, text_embed, image_grad, text_grads):
    return pl.pallas_call(
        backward_kernel,
        in_specs=[vmem] * 4,
        out_specs=[vmem] * 2,
        out_shape=[
            jax.ShapeDtypeStruct(image_embed.shape, jnp.bfloat16),
            jax.ShapeDtypeStruct(text_embed.shape, jnp.bfloat16),
        ],
        compiler_params=params(8),
    )(image_embed, text_embed, image_grad, text_grads)


def image_rings():
    depth, length, width, cores = SIZES
    rings = []
    for z in range(depth):
        for x in range(width):
            for c in range(cores):
                ring = [((z * length + y) * width + x) * cores + c for y in range(length)]
                rings.append(ring if c == 0 else ring[::-1])
    return rings


def exchanged(array):
    return lax.ppermute(array, "c", [(0, 1), (1, 0)])


def spread(copies, axis):
    return lax.all_to_all(copies, axis, split_axis=0, concat_axis=0, tiled=True).reshape(-1, copies.shape[2])


def parted(rows, axis):
    parts = rows.reshape(lax.axis_size(axis), -1, rows.shape[1])
    return lax.all_to_all(parts, axis, split_axis=0, concat_axis=0, tiled=True)


def on_device(image_embed, text_embed, log_scale, logit_bias, pair_index):
    own_images = image_embed.shape[0]
    rings = image_rings()
    images = lax.all_gather(image_embed, AXES, axis=0, tiled=True, axis_index_groups=rings)

    texts = spread(text_packets(pair_index, text_embed, lax.axis_size("z")), "z")
    own = spread(jnp.broadcast_to(texts[None], (lax.axis_size("x"),) + texts.shape), "x")
    other = exchanged(own)

    scale = jnp.exp(log_scale)
    scalars = jnp.concatenate([scale, -math.log2(math.e) * scale, -math.log2(math.e) * logit_bias])
    z, x, c = lax.axis_index("z"), lax.axis_index("x"), lax.axis_index("c")
    place = jnp.arange(SIZES[1], dtype=jnp.int32)
    place = jnp.where(c == 0, place, SIZES[1] - 1 - place)
    first = (((z * SIZES[1] + place) * SIZES[2] + x) * SIZES[3] + c) * own_images

    image_part, weights, units = weights_and_image_terms(first.astype(jnp.int32), scalars, images, own, other)
    image_grad = lax.psum_scatter(image_part, AXES, scatter_dimension=0, tiled=True, axis_index_groups=rings)

    own_part, other_part = text_terms(weights, units)
    text_part = own_part.astype(jnp.float32) + exchanged(other_part).astype(jnp.float32)
    text_part = jnp.sum(parted(text_part.astype(jnp.bfloat16), "x").astype(jnp.float32), axis=0)
    text_grads = parted(text_part.astype(jnp.bfloat16), "z")
    return unit_backward(image_embed, text_embed, image_grad, text_grads)


def solution(mesh):
    split = Mesh(mesh.devices.reshape(SIZES), AXES)
    rows = P(AXES, None)
    return jax.shard_map(
        on_device,
        mesh=split,
        in_specs=(rows, rows, P(), P(), P(AXES)),
        out_specs=(rows, rows),
        check_vma=False,
    )
```

```python
import math

import jax
import jax.numpy as jnp
from jax import lax
from jax.experimental import pallas as pl
from jax.experimental.pallas import tpu as pltpu
from jax.sharding import Mesh
from jax.sharding import PartitionSpec as P

AXES = ("z", "y", "x", "c")
SIZES = (8, 8, 4, 2)
LANES = 128
MIB = 1024 * 1024
ROWS_BY_ROWS = (((1,), (1,)), ((), ()))
COLUMNS_BY_ROWS = (((0,), (0,)), ((), ()))

smem = pl.BlockSpec(memory_space=pltpu.SMEM)
vmem = pl.BlockSpec(memory_space=pltpu.VMEM)
hbm = pl.BlockSpec(memory_space=pltpu.HBM)


def params(mib):
    return pltpu.CompilerParams(vmem_limit_bytes=mib * MIB)


def inverse_norm(floats):
    return lax.rsqrt(jnp.sum(floats * floats, axis=-1, keepdims=True) + 1e-06)


def unit_kernel(pair_ref, image_ref, text_ref, unit_ref, packet_ref):
    floats = image_ref[...].astype(jnp.float32)
    unit_ref[...] = (floats * inverse_norm(floats)).astype(unit_ref.dtype)
    rows, width = text_ref.shape
    floats = text_ref[...].astype(jnp.float32)
    unit = (floats * inverse_norm(floats)).astype(packet_ref.dtype)
    row = lax.broadcasted_iota(jnp.int32, (rows, LANES), 0)
    lane = lax.broadcasted_iota(jnp.int32, (rows, LANES), 1)
    index = jnp.zeros((rows, LANES), jnp.int32)
    for i in range(rows):
        index = jnp.where(row == i, pair_ref[i], index)
    digits = jnp.where(lane == 0, index >> 8, jnp.where(lane == 1, index & 255, 0))
    digits = digits.astype(jnp.float32).astype(packet_ref.dtype)
    for peer in range(packet_ref.shape[0]):
        packet_ref[peer, :, :width] = unit
        packet_ref[peer, :, width:] = digits


def units_and_packets(pair_index, image_embed, text_embed, peers):
    rows, width = text_embed.shape
    return pl.pallas_call(
        unit_kernel,
        in_specs=[smem, vmem, vmem],
        out_specs=[vmem, vmem],
        out_shape=[
            jax.ShapeDtypeStruct(image_embed.shape, jnp.bfloat16),
            jax.ShapeDtypeStruct((peers, rows, width + LANES), jnp.bfloat16),
        ],
        compiler_params=params(56),
    )(pair_index, image_embed, text_embed)


def weight_kernel(first_ref, scalars_ref, images_ref, own_ref, other_ref, *refs):
    image_grad_ref, weights_ref, image_ref, text_ref, weight_ref, grad_ref, sems = refs
    arrival = pltpu.make_async_copy(images_ref, image_ref, sems.at[0])
    arrival.start()
    rows, width = image_ref.shape
    count = own_ref.shape[0]
    text_ref[:count, :] = own_ref[...]
    text_ref[count:, :] = other_ref[...]
    digits = text_ref[:, width:].astype(jnp.float32).T
    pairs = (digits[0:1] * 256.0 + digits[1:2]).astype(jnp.int32)
    row = lax.broadcasted_iota(jnp.int32, (128, 1), 0)
    places = jnp.concatenate([row + first_ref[p] for p in range(rows // 128)], axis=0)
    texts = text_ref[:, :width]
    arrival.wait()
    dots = lax.dot_general(image_ref[...], texts, ROWS_BY_ROWS, preferred_element_type=jnp.float32)
    chance = 1.0 / (1.0 + jnp.exp2(dots * scalars_ref[1] + scalars_ref[2]))
    weight = (scalars_ref[0] * jnp.where(pairs == places, chance - 1.0, chance)).astype(jnp.bfloat16)
    weight_ref[...] = weight
    leaving = [pltpu.make_async_copy(weight_ref, weights_ref, sems.at[1])]
    leaving[0].start()
    half = rows // 2
    for i in range(2):
        part = pl.ds(i * half, half)
        grad = jnp.dot(weight[i * half : (i + 1) * half], texts, preferred_element_type=jnp.float32)
        grad_ref[part, :] = grad.astype(grad_ref.dtype)
        leaving.append(pltpu.make_async_copy(grad_ref.at[part], image_grad_ref.at[part], sems.at[2 + i]))
        leaving[-1].start()
    for copy in leaving:
        copy.wait()


def weights_and_image_terms(first, scalars, images, own, other):
    rows, width = images.shape
    count, wide = own.shape
    texts = 2 * count
    return pl.pallas_call(
        weight_kernel,
        in_specs=[smem, smem, hbm, vmem, vmem],
        out_specs=[hbm] * 2,
        out_shape=[
            jax.ShapeDtypeStruct((rows, width), jnp.bfloat16),
            jax.ShapeDtypeStruct((rows, texts), jnp.bfloat16),
        ],
        scratch_shapes=[
            pltpu.VMEM((rows, width), jnp.bfloat16),
            pltpu.VMEM((texts, wide), jnp.bfloat16),
            pltpu.VMEM((rows, texts), jnp.bfloat16),
            pltpu.VMEM((rows, width), jnp.bfloat16),
            pltpu.SemaphoreType.DMA((4,)),
        ],
        compiler_params=params(32),
        cost_estimate=pl.CostEstimate(
            flops=4 * rows * texts * width, bytes_accessed=4 * (rows + texts) * width, transcendentals=2 * rows * texts
        ),
    )(first, scalars, images, own, other)


def text_kernel(weights_ref, images_ref, own_grad_ref, other_grad_ref, weight_ref, image_ref, sems):
    copies = [
        pltpu.make_async_copy(weights_ref, weight_ref, sems.at[0]),
        pltpu.make_async_copy(images_ref, image_ref, sems.at[1]),
    ]
    for copy in copies:
        copy.start()
    for copy in copies:
        copy.wait()
    count = own_grad_ref.shape[0]
    grad = lax.dot_general(weight_ref[...], image_ref[...], COLUMNS_BY_ROWS, preferred_element_type=jnp.float32)
    own_grad_ref[...] = grad[:count].astype(own_grad_ref.dtype)
    other_grad_ref[...] = grad[count:].astype(other_grad_ref.dtype)


def text_terms(weights, images):
    rows, texts = weights.shape
    width = images.shape[1]
    return pl.pallas_call(
        text_kernel,
        in_specs=[hbm] * 2,
        out_specs=[vmem] * 2,
        out_shape=[jax.ShapeDtypeStruct((texts // 2, width), jnp.bfloat16)] * 2,
        scratch_shapes=[
            pltpu.VMEM(weights.shape, jnp.bfloat16),
            pltpu.VMEM(images.shape, jnp.bfloat16),
            pltpu.SemaphoreType.DMA((2,)),
        ],
        compiler_params=params(24),
        cost_estimate=pl.CostEstimate(
            flops=2 * rows * texts * width, bytes_accessed=2 * (rows + texts) * width, transcendentals=0
        ),
    )(weights, images)


def project(embed_ref, grad, out_ref):
    floats = embed_ref[...].astype(jnp.float32)
    inverse = inverse_norm(floats)
    unit = floats * inverse
    along = jnp.sum(unit * grad, axis=-1, keepdims=True)
    out_ref[...] = ((grad - unit * along) * inverse).astype(out_ref.dtype)


def backward_kernel(image_ref, text_ref, image_grads_ref, text_grads_ref, image_out_ref, text_out_ref, image_grad_ref, sem):
    copy = pltpu.make_async_copy(image_grads_ref, image_grad_ref, sem)
    copy.start()
    text_grad = text_grads_ref[0].astype(jnp.float32)
    for part in range(1, text_grads_ref.shape[0]):
        text_grad += text_grads_ref[part].astype(jnp.float32)
    project(text_ref, text_grad, text_out_ref)
    copy.wait()
    project(image_ref, image_grad_ref[...].astype(jnp.float32), image_out_ref)


def unit_backward(image_embed, text_embed, image_grad, text_grads):
    return pl.pallas_call(
        backward_kernel,
        in_specs=[vmem, vmem, hbm, vmem],
        out_specs=[vmem] * 2,
        out_shape=[
            jax.ShapeDtypeStruct(image_embed.shape, jnp.bfloat16),
            jax.ShapeDtypeStruct(text_embed.shape, jnp.bfloat16),
        ],
        scratch_shapes=[pltpu.VMEM(image_grad.shape, image_grad.dtype), pltpu.SemaphoreType.DMA],
        compiler_params=params(8),
    )(image_embed, text_embed, image_grad, text_grads)


def image_rings():
    depth, length, width, cores = SIZES
    rings = []
    for z in range(depth):
        for x in range(width):
            for c in range(cores):
                ring = [((z * length + y) * width + x) * cores + c for y in range(length)]
                rings.append(ring if c == 0 else ring[::-1])
    return rings


def exchanged(array):
    return lax.ppermute(array, "c", [(0, 1), (1, 0)])


def spread(copies, axis):
    return lax.all_to_all(copies, axis, split_axis=0, concat_axis=0, tiled=True).reshape(-1, copies.shape[2])


def parted(rows, axis):
    parts = rows.reshape(lax.axis_size(axis), -1, rows.shape[1])
    return lax.all_to_all(parts, axis, split_axis=0, concat_axis=0, tiled=True)


def on_device(image_embed, text_embed, log_scale, logit_bias, pair_index):
    own_images = image_embed.shape[0]
    rings = image_rings()
    unit, packets = units_and_packets(pair_index, image_embed, text_embed, lax.axis_size("z"))
    images = lax.all_gather(unit, AXES, axis=0, tiled=True, axis_index_groups=rings)

    texts = spread(packets, "z")
    own = spread(jnp.broadcast_to(texts[None], (lax.axis_size("x"),) + texts.shape), "x")
    other = exchanged(own)

    scale = jnp.exp(log_scale)
    scalars = jnp.concatenate([scale, -math.log2(math.e) * scale, -math.log2(math.e) * logit_bias])
    z, x, c = lax.axis_index("z"), lax.axis_index("x"), lax.axis_index("c")
    place = jnp.arange(SIZES[1], dtype=jnp.int32)
    place = jnp.where(c == 0, place, SIZES[1] - 1 - place)
    first = (((z * SIZES[1] + place) * SIZES[2] + x) * SIZES[3] + c) * own_images

    image_part, weights = weights_and_image_terms(first.astype(jnp.int32), scalars, images, own, other)
    image_grad = lax.psum_scatter(image_part, AXES, scatter_dimension=0, tiled=True, axis_index_groups=rings)

    own_part, other_part = text_terms(weights, images)
    text_part = own_part.astype(jnp.float32) + exchanged(other_part).astype(jnp.float32)
    text_part = jnp.sum(parted(text_part.astype(jnp.bfloat16), "x").astype(jnp.float32), axis=0)
    text_grads = parted(text_part.astype(jnp.bfloat16), "z")
    return unit_backward(image_embed, text_embed, image_grad, text_grads)


def solution(mesh):
    split = Mesh(mesh.devices.reshape(SIZES), AXES)
    rows = P(AXES, None)
    return jax.shard_map(
        on_device,
        mesh=split,
        in_specs=(rows, rows, P(), P(), P(AXES)),
        out_specs=(rows, rows),
        check_vma=False,
    )
```

```python
import math

import jax
import jax.numpy as jnp
from jax import lax
from jax.experimental import pallas as pl
from jax.experimental.pallas import tpu as pltpu
from jax.sharding import Mesh
from jax.sharding import PartitionSpec as P

AXES = ("z", "y", "x", "c")
SIZES = (8, 8, 4, 2)
LANES = 128
MIB = 1024 * 1024
ROWS_BY_ROWS = (((1,), (1,)), ((), ()))
COLUMNS_BY_ROWS = (((0,), (0,)), ((), ()))

smem = pl.BlockSpec(memory_space=pltpu.SMEM)
vmem = pl.BlockSpec(memory_space=pltpu.VMEM)
hbm = pl.BlockSpec(memory_space=pltpu.HBM)


def params(mib):
    return pltpu.CompilerParams(vmem_limit_bytes=mib * MIB)


def inverse_norm(floats):
    return lax.rsqrt(jnp.sum(floats * floats, axis=-1, keepdims=True) + 1e-06)


def unit_kernel(pair_ref, image_ref, text_ref, unit_ref, packet_ref):
    floats = image_ref[...].astype(jnp.float32)
    unit_ref[...] = (floats * inverse_norm(floats)).astype(unit_ref.dtype)
    rows, width = text_ref.shape
    floats = text_ref[...].astype(jnp.float32)
    unit = (floats * inverse_norm(floats)).astype(packet_ref.dtype)
    row = lax.broadcasted_iota(jnp.int32, (rows, LANES), 0)
    lane = lax.broadcasted_iota(jnp.int32, (rows, LANES), 1)
    index = jnp.zeros((rows, LANES), jnp.int32)
    for i in range(rows):
        index = jnp.where(row == i, pair_ref[i], index)
    digits = jnp.where(lane == 0, index >> 8, jnp.where(lane == 1, index & 255, 0))
    digits = digits.astype(jnp.float32).astype(packet_ref.dtype)
    for peer in range(packet_ref.shape[0]):
        packet_ref[peer, :, :width] = unit
        packet_ref[peer, :, width:] = digits


def units_and_packets(pair_index, image_embed, text_embed, peers):
    rows, width = text_embed.shape
    return pl.pallas_call(
        unit_kernel,
        in_specs=[smem, vmem, vmem],
        out_specs=[vmem, vmem],
        out_shape=[
            jax.ShapeDtypeStruct(image_embed.shape, jnp.bfloat16),
            jax.ShapeDtypeStruct((peers, rows, width + LANES), jnp.bfloat16),
        ],
        compiler_params=params(56),
    )(pair_index, image_embed, text_embed)


def weight_kernel(first_ref, scalars_ref, images_ref, own_ref, other_ref, *refs):
    image_grad_ref, weights_ref, image_ref, text_ref, weight_ref, grad_ref, sems = refs
    arrival = pltpu.make_async_copy(images_ref, image_ref, sems.at[0])
    arrival.start()
    rows, width = image_ref.shape
    count = own_ref.shape[0]
    text_ref[:count, :] = own_ref[...]
    text_ref[count:, :] = other_ref[...]
    digits = text_ref[:, width:].astype(jnp.float32).T
    pairs = (digits[0:1] * 256.0 + digits[1:2]).astype(jnp.int32)
    row = lax.broadcasted_iota(jnp.int32, (128, 1), 0)
    places = jnp.concatenate([row + first_ref[p] for p in range(rows // 128)], axis=0)
    texts = text_ref[:, :width]
    arrival.wait()
    dots = lax.dot_general(image_ref[...], texts, ROWS_BY_ROWS, preferred_element_type=jnp.float32)
    chance = 1.0 / (1.0 + jnp.exp2(dots * scalars_ref[1] + scalars_ref[2]))
    weight = (scalars_ref[0] * jnp.where(pairs == places, chance - 1.0, chance)).astype(jnp.bfloat16)
    weight_ref[...] = weight
    leaving = [pltpu.make_async_copy(weight_ref, weights_ref, sems.at[1])]
    leaving[0].start()
    half = rows // 2
    for i in range(2):
        part = pl.ds(i * half, half)
        grad = jnp.dot(weight[i * half : (i + 1) * half], texts, preferred_element_type=jnp.float32)
        grad_ref[part, :] = grad.astype(grad_ref.dtype)
        leaving.append(pltpu.make_async_copy(grad_ref.at[part], image_grad_ref.at[part], sems.at[2 + i]))
        leaving[-1].start()
    for copy in leaving:
        copy.wait()


def weights_and_image_terms(first, scalars, images, own, other):
    rows, width = images.shape
    count, wide = own.shape
    texts = 2 * count
    return pl.pallas_call(
        weight_kernel,
        in_specs=[smem, smem, hbm, vmem, vmem],
        out_specs=[hbm] * 2,
        out_shape=[
            jax.ShapeDtypeStruct((rows, width), jnp.bfloat16),
            jax.ShapeDtypeStruct((rows, texts), jnp.bfloat16),
        ],
        scratch_shapes=[
            pltpu.VMEM((rows, width), jnp.bfloat16),
            pltpu.VMEM((texts, wide), jnp.bfloat16),
            pltpu.VMEM((rows, texts), jnp.bfloat16),
            pltpu.VMEM((rows, width), jnp.bfloat16),
            pltpu.SemaphoreType.DMA((4,)),
        ],
        compiler_params=params(58),
        cost_estimate=pl.CostEstimate(
            flops=4 * rows * texts * width, bytes_accessed=4 * (rows + texts) * width, transcendentals=2 * rows * texts
        ),
    )(first, scalars, images, own, other)


def text_kernel(weights_ref, images_ref, own_grad_ref, other_grad_ref, weight_ref, image_ref, sems):
    copies = [
        pltpu.make_async_copy(weights_ref, weight_ref, sems.at[0]),
        pltpu.make_async_copy(images_ref, image_ref, sems.at[1]),
    ]
    for copy in copies:
        copy.start()
    for copy in copies:
        copy.wait()
    count = own_grad_ref.shape[0]
    grad = lax.dot_general(weight_ref[...], image_ref[...], COLUMNS_BY_ROWS, preferred_element_type=jnp.float32)
    own_grad_ref[...] = grad[:count].astype(own_grad_ref.dtype)
    other_grad_ref[...] = grad[count:].astype(other_grad_ref.dtype)


def text_terms(weights, images):
    rows, texts = weights.shape
    width = images.shape[1]
    return pl.pallas_call(
        text_kernel,
        in_specs=[hbm] * 2,
        out_specs=[vmem] * 2,
        out_shape=[jax.ShapeDtypeStruct((texts // 2, width), jnp.bfloat16)] * 2,
        scratch_shapes=[
            pltpu.VMEM(weights.shape, jnp.bfloat16),
            pltpu.VMEM(images.shape, jnp.bfloat16),
            pltpu.SemaphoreType.DMA((2,)),
        ],
        compiler_params=params(58),
        cost_estimate=pl.CostEstimate(
            flops=2 * rows * texts * width, bytes_accessed=2 * (rows + texts) * width, transcendentals=0
        ),
    )(weights, images)


def project(embed_ref, grad, out_ref):
    floats = embed_ref[...].astype(jnp.float32)
    inverse = inverse_norm(floats)
    unit = floats * inverse
    along = jnp.sum(unit * grad, axis=-1, keepdims=True)
    out_ref[...] = ((grad - unit * along) * inverse).astype(out_ref.dtype)


def backward_kernel(image_ref, text_ref, image_grads_ref, text_grads_ref, image_out_ref, text_out_ref, image_grad_ref, sem):
    copy = pltpu.make_async_copy(image_grads_ref, image_grad_ref, sem)
    copy.start()
    text_grad = text_grads_ref[0].astype(jnp.float32)
    for part in range(1, text_grads_ref.shape[0]):
        text_grad += text_grads_ref[part].astype(jnp.float32)
    project(text_ref, text_grad, text_out_ref)
    copy.wait()
    project(image_ref, image_grad_ref[...].astype(jnp.float32), image_out_ref)


def unit_backward(image_embed, text_embed, image_grad, text_grads):
    return pl.pallas_call(
        backward_kernel,
        in_specs=[vmem, vmem, hbm, vmem],
        out_specs=[vmem] * 2,
        out_shape=[
            jax.ShapeDtypeStruct(image_embed.shape, jnp.bfloat16),
            jax.ShapeDtypeStruct(text_embed.shape, jnp.bfloat16),
        ],
        scratch_shapes=[pltpu.VMEM(image_grad.shape, image_grad.dtype), pltpu.SemaphoreType.DMA],
        compiler_params=params(8),
    )(image_embed, text_embed, image_grad, text_grads)


def image_rings():
    depth, length, width, cores = SIZES
    rings = []
    for z in range(depth):
        for x in range(width):
            for c in range(cores):
                ring = [((z * length + y) * width + x) * cores + c for y in range(length)]
                rings.append(ring if c == 0 else ring[::-1])
    return rings


def exchanged(array):
    return lax.ppermute(array, "c", [(0, 1), (1, 0)])


def spread(copies, axis):
    return lax.all_to_all(copies, axis, split_axis=0, concat_axis=0, tiled=True).reshape(-1, copies.shape[2])


def parted(rows, axis):
    parts = rows.reshape(lax.axis_size(axis), -1, rows.shape[1])
    return lax.all_to_all(parts, axis, split_axis=0, concat_axis=0, tiled=True)


def on_device(image_embed, text_embed, log_scale, logit_bias, pair_index):
    own_images = image_embed.shape[0]
    rings = image_rings()
    unit, packets = units_and_packets(pair_index, image_embed, text_embed, lax.axis_size("z"))
    images = lax.all_gather(unit, AXES, axis=0, tiled=True, axis_index_groups=rings)

    texts = spread(packets, "z")
    own = spread(jnp.broadcast_to(texts[None], (lax.axis_size("x"),) + texts.shape), "x")
    other = exchanged(own)

    scale = jnp.exp(log_scale)
    scalars = jnp.concatenate([scale, -math.log2(math.e) * scale, -math.log2(math.e) * logit_bias])
    z, x, c = lax.axis_index("z"), lax.axis_index("x"), lax.axis_index("c")
    place = jnp.arange(SIZES[1], dtype=jnp.int32)
    place = jnp.where(c == 0, place, SIZES[1] - 1 - place)
    first = (((z * SIZES[1] + place) * SIZES[2] + x) * SIZES[3] + c) * own_images

    image_part, weights = weights_and_image_terms(first.astype(jnp.int32), scalars, images, own, other)
    image_grad = lax.psum_scatter(image_part, AXES, scatter_dimension=0, tiled=True, axis_index_groups=rings)

    own_part, other_part = text_terms(weights, images)
    text_part = own_part.astype(jnp.float32) + exchanged(other_part).astype(jnp.float32)
    text_part = jnp.sum(parted(text_part.astype(jnp.bfloat16), "x").astype(jnp.float32), axis=0)
    text_grads = parted(text_part.astype(jnp.bfloat16), "z")
    return unit_backward(image_embed, text_embed, image_grad, text_grads)


def solution(mesh):
    split = Mesh(mesh.devices.reshape(SIZES), AXES)
    rows = P(AXES, None)
    return jax.shard_map(
        on_device,
        mesh=split,
        in_specs=(rows, rows, P(), P(), P(AXES)),
        out_specs=(rows, rows),
        check_vma=False,
    )
```

```python
import math

import jax
import jax.numpy as jnp
from jax import lax
from jax.experimental import pallas as pl
from jax.experimental.pallas import tpu as pltpu
from jax.sharding import Mesh
from jax.sharding import PartitionSpec as P

AXES = ("z", "y", "x", "c")
SIZES = (8, 8, 4, 2)
LANES = 128
PIECES = 4
MIB = 1024 * 1024
ROWS_BY_ROWS = (((1,), (1,)), ((), ()))
COLUMNS_BY_ROWS = (((0,), (0,)), ((), ()))

smem = pl.BlockSpec(memory_space=pltpu.SMEM)
vmem = pl.BlockSpec(memory_space=pltpu.VMEM)
hbm = pl.BlockSpec(memory_space=pltpu.HBM)


def params(mib):
    return pltpu.CompilerParams(vmem_limit_bytes=mib * MIB)


def inverse_norm(floats):
    return lax.rsqrt(jnp.sum(floats * floats, axis=-1, keepdims=True) + 1e-06)


def unit_kernel(embed_ref, unit_ref):
    floats = embed_ref[...].astype(jnp.float32)
    unit_ref[...] = (floats * inverse_norm(floats)).astype(unit_ref.dtype)


def units(embed):
    return pl.pallas_call(
        unit_kernel,
        in_specs=[vmem],
        out_specs=vmem,
        out_shape=jax.ShapeDtypeStruct(embed.shape, jnp.bfloat16),
        compiler_params=params(56),
    )(embed)


def packet_kernel(pair_ref, text_ref, packet_ref):
    rows, width = text_ref.shape
    floats = text_ref[...].astype(jnp.float32)
    unit = (floats * inverse_norm(floats)).astype(packet_ref.dtype)
    row = lax.broadcasted_iota(jnp.int32, (rows, LANES), 0)
    lane = lax.broadcasted_iota(jnp.int32, (rows, LANES), 1)
    index = jnp.zeros((rows, LANES), jnp.int32)
    for i in range(rows):
        index = jnp.where(row == i, pair_ref[i], index)
    digits = jnp.where(lane == 0, index >> 8, jnp.where(lane == 1, index & 255, 0))
    digits = digits.astype(jnp.float32).astype(packet_ref.dtype)
    for peer in range(packet_ref.shape[0]):
        packet_ref[peer, :, :width] = unit
        packet_ref[peer, :, width:] = digits


def text_packets(pair_index, embed, peers):
    rows, width = embed.shape
    return pl.pallas_call(
        packet_kernel,
        in_specs=[smem, vmem],
        out_specs=vmem,
        out_shape=jax.ShapeDtypeStruct((peers, rows, width + LANES), jnp.bfloat16),
        compiler_params=params(56),
    )(pair_index, embed)


def pair_kernel(first_ref, scalars_ref, images_ref, own_ref, other_ref, *refs):
    image_grads_ref, own_grad_ref, other_grad_ref, image_ref, text_ref, grad_ref, sems = refs
    height, width = image_ref.shape
    size = height // PIECES
    pieces = [pl.ds(i * size, size) for i in range(PIECES)]
    arriving = [pltpu.make_async_copy(images_ref.at[p], image_ref.at[p], sems.at[i]) for i, p in enumerate(pieces)]
    for copy in arriving:
        copy.start()
    count = own_ref.shape[0]
    text_ref[:count, :] = own_ref[...]
    text_ref[count:, :] = other_ref[...]
    digits = text_ref[:, width:].astype(jnp.float32).T
    pairs = (digits[0:1] * 256.0 + digits[1:2]).astype(jnp.int32)
    row = lax.broadcasted_iota(jnp.int32, (128, 1), 0)
    rows = jnp.concatenate([row + first_ref[p] for p in range(image_ref.shape[0] // 128)], axis=0)
    texts = text_ref[:, :width]
    for copy in arriving:
        copy.wait()
    images = image_ref[...]
    dots = lax.dot_general(images, texts, ROWS_BY_ROWS, preferred_element_type=jnp.float32)
    chance = 1.0 / (1.0 + jnp.exp2(dots * scalars_ref[1] + scalars_ref[2]))
    weight = (scalars_ref[0] * jnp.where(pairs == rows, chance - 1.0, chance)).astype(jnp.bfloat16)
    grad_ref[...] = jnp.dot(weight, texts, preferred_element_type=jnp.float32).astype(grad_ref.dtype)
    leaving = [pltpu.make_async_copy(grad_ref.at[p], image_grads_ref.at[p], sems.at[i]) for i, p in enumerate(pieces)]
    for copy in leaving:
        copy.start()
    text_grad = lax.dot_general(weight, images, COLUMNS_BY_ROWS, preferred_element_type=jnp.float32)
    own_grad_ref[...] = text_grad[:count].astype(own_grad_ref.dtype)
    other_grad_ref[...] = text_grad[count:].astype(other_grad_ref.dtype)
    for copy in leaving:
        copy.wait()


def pair_terms(first, scalars, images, own, other):
    rows, width = images.shape
    count, wide = own.shape
    texts = 2 * count
    return pl.pallas_call(
        pair_kernel,
        in_specs=[smem, smem, hbm, vmem, vmem],
        out_specs=[hbm, vmem, vmem],
        out_shape=[
            jax.ShapeDtypeStruct((rows, width), jnp.bfloat16),
            jax.ShapeDtypeStruct((count, width), jnp.bfloat16),
            jax.ShapeDtypeStruct((count, width), jnp.bfloat16),
        ],
        scratch_shapes=[
            pltpu.VMEM((rows, width), jnp.bfloat16),
            pltpu.VMEM((texts, wide), jnp.bfloat16),
            pltpu.VMEM((rows, width), jnp.bfloat16),
            pltpu.SemaphoreType.DMA((PIECES,)),
        ],
        compiler_params=params(48),
        cost_estimate=pl.CostEstimate(
            flops=6 * rows * texts * width, bytes_accessed=4 * (rows + texts) * width, transcendentals=2 * rows * texts
        ),
    )(first, scalars, images, own, other)


def project(embed_ref, grad, out_ref):
    floats = embed_ref[...].astype(jnp.float32)
    inverse = inverse_norm(floats)
    unit = floats * inverse
    along = jnp.sum(unit * grad, axis=-1, keepdims=True)
    out_ref[...] = ((grad - unit * along) * inverse).astype(out_ref.dtype)


def backward_kernel(image_ref, text_ref, image_grad_ref, text_grads_ref, image_out_ref, text_out_ref):
    project(image_ref, image_grad_ref[...].astype(jnp.float32), image_out_ref)
    text_grad = text_grads_ref[0].astype(jnp.float32)
    for part in range(1, text_grads_ref.shape[0]):
        text_grad += text_grads_ref[part].astype(jnp.float32)
    project(text_ref, text_grad, text_out_ref)


def unit_backward(image_embed, text_embed, image_grad, text_grads):
    return pl.pallas_call(
        backward_kernel,
        in_specs=[vmem] * 4,
        out_specs=[vmem] * 2,
        out_shape=[
            jax.ShapeDtypeStruct(image_embed.shape, jnp.bfloat16),
            jax.ShapeDtypeStruct(text_embed.shape, jnp.bfloat16),
        ],
        compiler_params=params(8),
    )(image_embed, text_embed, image_grad, text_grads)


def image_rings():
    depth, length, width, cores = SIZES
    rings = []
    for z in range(depth):
        for x in range(width):
            for c in range(cores):
                ring = [((z * length + y) * width + x) * cores + c for y in range(length)]
                rings.append(ring if c == 0 else ring[::-1])
    return rings


def exchanged(array):
    return lax.ppermute(array, "c", [(0, 1), (1, 0)])


def spread(copies, axis):
    return lax.all_to_all(copies, axis, split_axis=0, concat_axis=0, tiled=True).reshape(-1, copies.shape[2])


def parted(rows, axis):
    parts = rows.reshape(lax.axis_size(axis), -1, rows.shape[1])
    return lax.all_to_all(parts, axis, split_axis=0, concat_axis=0, tiled=True)


def on_device(image_embed, text_embed, log_scale, logit_bias, pair_index):
    own_images = image_embed.shape[0]
    rings = image_rings()
    images = lax.all_gather(units(image_embed), AXES, axis=0, tiled=True, axis_index_groups=rings)

    texts = spread(text_packets(pair_index, text_embed, lax.axis_size("z")), "z")
    own = spread(jnp.broadcast_to(texts[None], (lax.axis_size("x"),) + texts.shape), "x")
    other = exchanged(own)

    scale = jnp.exp(log_scale)
    scalars = jnp.concatenate([scale, -math.log2(math.e) * scale, -math.log2(math.e) * logit_bias])
    z, x, c = lax.axis_index("z"), lax.axis_index("x"), lax.axis_index("c")
    place = jnp.arange(SIZES[1], dtype=jnp.int32)
    place = jnp.where(c == 0, place, SIZES[1] - 1 - place)
    first = (((z * SIZES[1] + place) * SIZES[2] + x) * SIZES[3] + c) * own_images

    image_part, own_part, other_part = pair_terms(first.astype(jnp.int32), scalars, images, own, other)
    image_grad = lax.psum_scatter(image_part, AXES, scatter_dimension=0, tiled=True, axis_index_groups=rings)

    text_part = own_part.astype(jnp.float32) + exchanged(other_part).astype(jnp.float32)
    text_part = jnp.sum(parted(text_part.astype(jnp.bfloat16), "x").astype(jnp.float32), axis=0)
    text_grads = parted(text_part.astype(jnp.bfloat16), "z")
    return unit_backward(image_embed, text_embed, image_grad, text_grads)


def solution(mesh):
    split = Mesh(mesh.devices.reshape(SIZES), AXES)
    rows = P(AXES, None)
    return jax.shard_map(
        on_device,
        mesh=split,
        in_specs=(rows, rows, P(), P(), P(AXES)),
        out_specs=(rows, rows),
        check_vma=False,
    )
```

```python
import math

import jax
import jax.numpy as jnp
from jax import lax
from jax.experimental import pallas as pl
from jax.experimental.pallas import tpu as pltpu
from jax.sharding import Mesh
from jax.sharding import PartitionSpec as P

AXES = ("z", "y", "x", "c")
SIZES = (8, 8, 4, 2)
FAR = ("z", "y")
MIB = 1024 * 1024
ROWS_BY_ROWS = (((1,), (1,)), ((), ()))
COLUMNS_BY_ROWS = (((0,), (0,)), ((), ()))

smem = pl.BlockSpec(memory_space=pltpu.SMEM)
vmem = pl.BlockSpec(memory_space=pltpu.VMEM)


def params(mib):
    return pltpu.CompilerParams(vmem_limit_bytes=mib * MIB)


def inverse_norm(floats):
    return lax.rsqrt(jnp.sum(floats * floats, axis=-1, keepdims=True) + 1e-06)


def unit_kernel(image_ref, text_ref, unit_ref, copies_ref):
    floats = image_ref[...].astype(jnp.float32)
    unit_ref[...] = (floats * inverse_norm(floats)).astype(unit_ref.dtype)
    floats = text_ref[...].astype(jnp.float32)
    unit = (floats * inverse_norm(floats)).astype(copies_ref.dtype)
    for peer in range(copies_ref.shape[0]):
        copies_ref[peer] = unit


def units_and_copies(image_embed, text_embed, peers):
    return pl.pallas_call(
        unit_kernel,
        in_specs=[vmem] * 2,
        out_specs=[vmem] * 2,
        out_shape=[
            jax.ShapeDtypeStruct(image_embed.shape, jnp.bfloat16),
            jax.ShapeDtypeStruct((peers,) + text_embed.shape, jnp.bfloat16),
        ],
        compiler_params=params(56),
    )(image_embed, text_embed)


def weight_kernel(first_ref, scalars_ref, own_ref, other_ref, text_ref, pair_ref, weight_ref, grad_ref, image_ref):
    half = own_ref.shape[0]
    image_ref[:half, :] = own_ref[...]
    image_ref[half:, :] = other_ref[...]
    row = lax.broadcasted_iota(jnp.int32, (128, 1), 0)
    places = jnp.concatenate([row + first_ref[p] for p in range(2 * half // 128)], axis=0)
    images = image_ref[...]
    dots = lax.dot_general(images, text_ref[...], ROWS_BY_ROWS, preferred_element_type=jnp.float32)
    chance = 1.0 / (1.0 + jnp.exp2(dots * scalars_ref[1] + scalars_ref[2]))
    weight = (scalars_ref[0] * jnp.where(pair_ref[...] == places, chance - 1.0, chance)).astype(jnp.bfloat16)
    weight_ref[...] = weight
    grad = lax.dot_general(weight, images, COLUMNS_BY_ROWS, preferred_element_type=jnp.float32)
    grad_ref[...] = grad.astype(grad_ref.dtype)


def weights_and_text_terms(first, scalars, own, other, texts, pairs):
    half, width = own.shape
    count = texts.shape[0]
    return pl.pallas_call(
        weight_kernel,
        in_specs=[smem, smem] + [vmem] * 4,
        out_specs=[vmem] * 2,
        out_shape=[
            jax.ShapeDtypeStruct((2 * half, count), jnp.bfloat16),
            jax.ShapeDtypeStruct((count, width), jnp.bfloat16),
        ],
        scratch_shapes=[pltpu.VMEM((2 * half, width), jnp.bfloat16)],
        compiler_params=params(32),
        cost_estimate=pl.CostEstimate(
            flops=8 * half * count * width,
            bytes_accessed=4 * (half + count) * width + 4 * half * count,
            transcendentals=4 * half * count,
        ),
    )(first, scalars, own, other, texts, pairs)


def image_kernel(weight_ref, text_ref, own_ref, other_ref):
    grad = jnp.dot(weight_ref[...], text_ref[...], preferred_element_type=jnp.float32)
    half = own_ref.shape[0]
    own_ref[...] = grad[:half].astype(own_ref.dtype)
    other_ref[...] = grad[half:].astype(other_ref.dtype)


def image_terms(weights, texts):
    rows, count = weights.shape
    width = texts.shape[1]
    return pl.pallas_call(
        image_kernel,
        in_specs=[vmem] * 2,
        out_specs=[vmem] * 2,
        out_shape=[jax.ShapeDtypeStruct((rows // 2, width), jnp.bfloat16)] * 2,
        compiler_params=params(24),
        cost_estimate=pl.CostEstimate(
            flops=2 * rows * count * width, bytes_accessed=2 * (rows + count) * width + 2 * rows * count, transcendentals=0
        ),
    )(weights, texts)


def backward_kernel(embed_ref, *refs):
    floats = embed_ref[...].astype(jnp.float32)
    inverse = inverse_norm(floats)
    unit = floats * inverse
    parts_refs, out_ref = refs[:-1], refs[-1]
    grad = None
    for ref in parts_refs:
        for part in [ref[...]] if len(ref.shape) == 2 else [ref[i] for i in range(ref.shape[0])]:
            part = part.astype(jnp.float32)
            grad = part if grad is None else grad + part
    along = jnp.sum(unit * grad, axis=-1, keepdims=True)
    out_ref[...] = ((grad - unit * along) * inverse).astype(out_ref.dtype)


def unit_backward(embed, *parts):
    return pl.pallas_call(
        backward_kernel,
        in_specs=[vmem] * (1 + len(parts)),
        out_specs=vmem,
        out_shape=jax.ShapeDtypeStruct(embed.shape, jnp.bfloat16),
        compiler_params=params(8),
    )(embed, *parts)


def shifted(array, axis, by):
    devices = lax.axis_size(axis)
    return lax.ppermute(array, axis, [(i, (i + by) % devices) for i in range(devices)])


def on_device(image_embed, text_embed, log_scale, logit_bias, pair_index):
    own_images, width = image_embed.shape
    own_texts = text_embed.shape[0]
    peers, ring = lax.axis_size(FAR), lax.axis_size("x")

    unit, copies = units_and_copies(image_embed, text_embed, peers)
    texts = lax.all_to_all(copies, FAR, split_axis=0, concat_axis=0, tiled=True).reshape(-1, width)
    pairs = lax.all_gather(pair_index, FAR, axis=0, tiled=True)
    own = lax.all_gather(unit, "x", axis=0, tiled=True)
    other = shifted(own, "c", 1)

    scale = jnp.exp(log_scale)
    scalars = jnp.concatenate([scale, -math.log2(math.e) * scale, -math.log2(math.e) * logit_bias])
    far, x, c = lax.axis_index(FAR), lax.axis_index("x"), lax.axis_index("c")
    first = jnp.stack(
        [((far * ring + place) * 2 + core) * own_images for core in (c, 1 - c) for place in range(ring)]
    ).astype(jnp.int32)
    weights, text_part = weights_and_text_terms(first, scalars, own, other, texts, pairs[None, :])
    text_parts = lax.all_to_all(
        text_part.reshape(peers, own_texts, width), FAR, split_axis=0, concat_axis=0, tiled=True
    )

    own_part, other_part = image_terms(weights, texts)
    part = own_part.astype(jnp.float32) + shifted(other_part, "c", 1).astype(jnp.float32)
    part = part.astype(jnp.bfloat16).reshape(ring, own_images, width)
    parts = [lax.dynamic_index_in_dim(part, (x + s) % ring, 0, keepdims=False) for s in range(ring)]
    parts = parts[:1] + [shifted(parts[s], "x", s) for s in range(1, ring)]
    return unit_backward(image_embed, *parts), unit_backward(text_embed, text_parts)


def solution(mesh):
    split = Mesh(mesh.devices.reshape(SIZES), AXES)
    rows = P(AXES, None)
    return jax.shard_map(
        on_device,
        mesh=split,
        in_specs=(rows, rows, P(), P(), P(AXES)),
        out_specs=(rows, rows),
        check_vma=False,
    )
```

```python
import math

import jax
import jax.numpy as jnp
from jax import lax
from jax.experimental import pallas as pl
from jax.experimental.pallas import tpu as pltpu
from jax.sharding import Mesh
from jax.sharding import PartitionSpec as P

AXES = ("z", "y", "x", "c")
SIZES = (8, 8, 4, 2)
FAR = ("z", "y")
LANES = 128
SUBLANES = 8
MIB = 1024 * 1024
ROWS_BY_ROWS = (((1,), (1,)), ((), ()))
COLUMNS_BY_ROWS = (((0,), (0,)), ((), ()))

smem = pl.BlockSpec(memory_space=pltpu.SMEM)
vmem = pl.BlockSpec(memory_space=pltpu.VMEM)
hbm = pl.BlockSpec(memory_space=pltpu.HBM)


def params(mib):
    return pltpu.CompilerParams(vmem_limit_bytes=mib * MIB)


def inverse_norm(floats):
    return lax.rsqrt(jnp.sum(floats * floats, axis=-1, keepdims=True) + 1e-06)


def unit_kernel(pair_ref, image_ref, text_ref, unit_ref, packet_ref):
    floats = image_ref[...].astype(jnp.float32)
    unit_ref[...] = (floats * inverse_norm(floats)).astype(unit_ref.dtype)
    rows, width = text_ref.shape
    floats = text_ref[...].astype(jnp.float32)
    unit = (floats * inverse_norm(floats)).astype(packet_ref.dtype)
    lane = lax.broadcasted_iota(jnp.int32, (SUBLANES, LANES), 1)
    digits = jnp.zeros((SUBLANES, LANES), jnp.int32)
    for i in range(rows):
        digits = jnp.where(lane == i, pair_ref[i] >> 8, digits)
        digits = jnp.where(lane == rows + i, pair_ref[i] & 255, digits)
    digits = digits.astype(jnp.float32).astype(packet_ref.dtype)
    blocks = width // LANES
    for peer in range(packet_ref.shape[0]):
        for k in range(blocks):
            packet_ref[peer, k * rows : (k + 1) * rows, :] = unit[:, k * LANES : (k + 1) * LANES]
        packet_ref[peer, blocks * rows :, :] = digits


def units_and_packets(pair_index, image_embed, text_embed, peers):
    rows, width = text_embed.shape
    return pl.pallas_call(
        unit_kernel,
        in_specs=[smem, vmem, vmem],
        out_specs=[vmem] * 2,
        out_shape=[
            jax.ShapeDtypeStruct(image_embed.shape, jnp.bfloat16),
            jax.ShapeDtypeStruct((peers, width // LANES * rows + SUBLANES, LANES), jnp.bfloat16),
        ],
        compiler_params=params(56),
    )(pair_index, image_embed, text_embed)


def pairs_of(digits, rows):
    count = digits.shape[0] // SUBLANES * rows
    lane = lax.broadcasted_iota(jnp.int32, (LANES, count), 0)
    text = lax.broadcasted_iota(jnp.int32, (LANES, count), 1) % rows
    place = jnp.where(lane == text, 256.0, jnp.where(lane == rows + text, 1.0, 0.0)).astype(jnp.bfloat16)
    spread = jnp.dot(digits, place, preferred_element_type=jnp.float32)
    tile = lax.broadcasted_iota(jnp.int32, spread.shape, 0)
    peer = lax.broadcasted_iota(jnp.int32, spread.shape, 1) // rows
    return jnp.sum(jnp.where(tile == peer * SUBLANES, spread, 0.0), axis=0, keepdims=True).astype(jnp.int32)


def put_texts(packet_ref, text_ref):
    blocks = text_ref.shape[1] // LANES
    rows = text_ref.shape[0] // packet_ref.shape[0]
    for k in range(blocks):
        block = packet_ref[:, k * rows : (k + 1) * rows, :]
        text_ref[:, k * LANES : (k + 1) * LANES] = block.reshape(text_ref.shape[0], LANES)
    return packet_ref[:, blocks * rows :, :].reshape(-1, LANES), rows


def weight_kernel(first_ref, scalars_ref, own_ref, other_ref, packet_ref, *refs):
    weights_ref, grads_ref, image_ref, text_ref, weight_ref, grad_ref, sems = refs
    half = own_ref.shape[0]
    image_ref[:half, :] = own_ref[...]
    image_ref[half:, :] = other_ref[...]
    pairs = pairs_of(*put_texts(packet_ref, text_ref))
    row = lax.broadcasted_iota(jnp.int32, (128, 1), 0)
    places = jnp.concatenate([row + first_ref[p] for p in range(2 * half // 128)], axis=0)
    images = image_ref[...]
    dots = lax.dot_general(images, text_ref[...], ROWS_BY_ROWS, preferred_element_type=jnp.float32)
    chance = 1.0 / (1.0 + jnp.exp2(dots * scalars_ref[1] + scalars_ref[2]))
    weight = (scalars_ref[0] * jnp.where(pairs == places, chance - 1.0, chance)).astype(jnp.bfloat16)
    weight_ref[...] = weight
    leaving = [pltpu.make_async_copy(weight_ref, weights_ref, sems.at[0])]
    leaving[0].start()
    grad = lax.dot_general(weight, images, COLUMNS_BY_ROWS, preferred_element_type=jnp.float32)
    grad_ref[...] = grad.astype(grad_ref.dtype)
    leaving.append(pltpu.make_async_copy(grad_ref, grads_ref, sems.at[1]))
    leaving[1].start()
    for copy in leaving:
        copy.wait()


def weights_and_text_terms(first, scalars, own, other, packets, rows):
    half, width = own.shape
    count = packets.shape[0] * rows
    return pl.pallas_call(
        weight_kernel,
        in_specs=[smem, smem] + [vmem] * 3,
        out_specs=[hbm, hbm],
        out_shape=[
            jax.ShapeDtypeStruct((2 * half, count), jnp.bfloat16),
            jax.ShapeDtypeStruct((count, width), jnp.bfloat16),
        ],
        scratch_shapes=[
            pltpu.VMEM((2 * half, width), jnp.bfloat16),
            pltpu.VMEM((count, width), jnp.bfloat16),
            pltpu.VMEM((2 * half, count), jnp.bfloat16),
            pltpu.VMEM((count, width), jnp.bfloat16),
            pltpu.SemaphoreType.DMA((2,)),
        ],
        compiler_params=params(48),
        cost_estimate=pl.CostEstimate(
            flops=8 * half * count * width,
            bytes_accessed=4 * (half + count) * width + 4 * half * count,
            transcendentals=4 * half * count,
        ),
    )(first, scalars, own, other, packets)


def image_kernel(weight_ref, packet_ref, own_ref, other_ref, text_ref):
    put_texts(packet_ref, text_ref)
    grad = jnp.dot(weight_ref[...], text_ref[...], preferred_element_type=jnp.float32)
    half = own_ref.shape[0]
    own_ref[...] = grad[:half].astype(own_ref.dtype)
    other_ref[...] = grad[half:].astype(other_ref.dtype)


def image_terms(weights, packets, width):
    rows, count = weights.shape
    return pl.pallas_call(
        image_kernel,
        in_specs=[vmem] * 2,
        out_specs=[vmem] * 2,
        out_shape=[jax.ShapeDtypeStruct((rows // 2, width), jnp.bfloat16)] * 2,
        scratch_shapes=[pltpu.VMEM((count, width), jnp.bfloat16)],
        compiler_params=params(24),
        cost_estimate=pl.CostEstimate(
            flops=2 * rows * count * width, bytes_accessed=2 * (rows + count) * width + 2 * rows * count, transcendentals=0
        ),
    )(weights, packets)


def backward_kernel(embed_ref, *refs):
    floats = embed_ref[...].astype(jnp.float32)
    inverse = inverse_norm(floats)
    unit = floats * inverse
    parts_refs, out_ref = refs[:-1], refs[-1]
    grad = None
    for ref in parts_refs:
        for part in [ref[...]] if len(ref.shape) == 2 else [ref[i] for i in range(ref.shape[0])]:
            part = part.astype(jnp.float32)
            grad = part if grad is None else grad + part
    along = jnp.sum(unit * grad, axis=-1, keepdims=True)
    out_ref[...] = ((grad - unit * along) * inverse).astype(out_ref.dtype)


def unit_backward(embed, *parts):
    return pl.pallas_call(
        backward_kernel,
        in_specs=[vmem] * (1 + len(parts)),
        out_specs=vmem,
        out_shape=jax.ShapeDtypeStruct(embed.shape, jnp.bfloat16),
        compiler_params=params(8),
    )(embed, *parts)


def shifted(array, axis, by):
    devices = lax.axis_size(axis)
    return lax.ppermute(array, axis, [(i, (i + by) % devices) for i in range(devices)])


def on_device(image_embed, text_embed, log_scale, logit_bias, pair_index):
    own_images, width = image_embed.shape
    own_texts = text_embed.shape[0]
    peers, ring = lax.axis_size(FAR), lax.axis_size("x")

    unit, packets = units_and_packets(pair_index, image_embed, text_embed, peers)
    packets = lax.all_to_all(packets, FAR, split_axis=0, concat_axis=0, tiled=True)
    own = lax.all_gather(unit, "x", axis=0, tiled=True)
    other = shifted(own, "c", 1)

    scale = jnp.exp(log_scale)
    scalars = jnp.concatenate([scale, -math.log2(math.e) * scale, -math.log2(math.e) * logit_bias])
    far, x, c = lax.axis_index(FAR), lax.axis_index("x"), lax.axis_index("c")
    first = jnp.stack(
        [((far * ring + place) * 2 + core) * own_images for core in (c, 1 - c) for place in range(ring)]
    ).astype(jnp.int32)
    weights, text_part = weights_and_text_terms(first, scalars, own, other, packets, own_texts)
    text_parts = lax.all_to_all(
        text_part.reshape(peers, own_texts, width), FAR, split_axis=0, concat_axis=0, tiled=True
    )

    own_part, other_part = image_terms(weights, packets, width)
    part = own_part.astype(jnp.float32) + shifted(other_part, "c", 1).astype(jnp.float32)
    part = part.astype(jnp.bfloat16).reshape(ring, own_images, width)
    parts = [lax.dynamic_index_in_dim(part, (x + s) % ring, 0, keepdims=False) for s in range(ring)]
    parts = parts[:1] + [shifted(parts[s], "x", s) for s in range(1, ring)]
    return unit_backward(image_embed, *parts), unit_backward(text_embed, text_parts)


def solution(mesh):
    split = Mesh(mesh.devices.reshape(SIZES), AXES)
    rows = P(AXES, None)
    return jax.shard_map(
        on_device,
        mesh=split,
        in_specs=(rows, rows, P(), P(), P(AXES)),
        out_specs=(rows, rows),
        check_vma=False,
    )
```

```python
import math

import jax
import jax.numpy as jnp
from jax import lax
from jax.experimental import pallas as pl
from jax.experimental.pallas import tpu as pltpu
from jax.sharding import Mesh
from jax.sharding import PartitionSpec as P

AXES = ("z", "yh", "ym", "yl", "x", "c")
SIZES = (8, 2, 2, 2, 4, 2)
FAR = ("z", "yh", "ym")
LANES = 128
SUBLANES = 8
MIB = 1024 * 1024
ROWS_BY_ROWS = (((1,), (1,)), ((), ()))
COLUMNS_BY_ROWS = (((0,), (0,)), ((), ()))

smem = pl.BlockSpec(memory_space=pltpu.SMEM)
vmem = pl.BlockSpec(memory_space=pltpu.VMEM)
hbm = pl.BlockSpec(memory_space=pltpu.HBM)


def params(mib):
    return pltpu.CompilerParams(vmem_limit_bytes=mib * MIB)


def inverse_norm(floats):
    return lax.rsqrt(jnp.sum(floats * floats, axis=-1, keepdims=True) + 1e-06)


def unit_kernel(pair_ref, image_ref, text_ref, unit_ref, packet_ref):
    floats = image_ref[...].astype(jnp.float32)
    unit_ref[...] = (floats * inverse_norm(floats)).astype(unit_ref.dtype)
    rows, width = text_ref.shape
    floats = text_ref[...].astype(jnp.float32)
    unit = (floats * inverse_norm(floats)).astype(packet_ref.dtype)
    lane = lax.broadcasted_iota(jnp.int32, (SUBLANES, LANES), 1)
    digits = jnp.zeros((SUBLANES, LANES), jnp.int32)
    for i in range(rows):
        digits = jnp.where(lane == i, pair_ref[i] >> 8, digits)
        digits = jnp.where(lane == rows + i, pair_ref[i] & 255, digits)
    digits = digits.astype(jnp.float32).astype(packet_ref.dtype)
    blocks = width // LANES
    for peer in range(packet_ref.shape[0]):
        for k in range(blocks):
            packet_ref[peer, k * rows : (k + 1) * rows, :] = unit[:, k * LANES : (k + 1) * LANES]
        packet_ref[peer, blocks * rows :, :] = digits


def units_and_packets(pair_index, image_embed, text_embed, peers):
    rows, width = text_embed.shape
    return pl.pallas_call(
        unit_kernel,
        in_specs=[smem, vmem, vmem],
        out_specs=[vmem] * 2,
        out_shape=[
            jax.ShapeDtypeStruct(image_embed.shape, jnp.bfloat16),
            jax.ShapeDtypeStruct((peers, width // LANES * rows + SUBLANES, LANES), jnp.bfloat16),
        ],
        compiler_params=params(56),
    )(pair_index, image_embed, text_embed)


def pairs_of(digits, rows):
    count = digits.shape[0] // SUBLANES * rows
    lane = lax.broadcasted_iota(jnp.int32, (LANES, count), 0)
    text = lax.broadcasted_iota(jnp.int32, (LANES, count), 1) % rows
    place = jnp.where(lane == text, 256.0, jnp.where(lane == rows + text, 1.0, 0.0)).astype(jnp.bfloat16)
    spread = jnp.dot(digits, place, preferred_element_type=jnp.float32)
    tile = lax.broadcasted_iota(jnp.int32, spread.shape, 0)
    peer = lax.broadcasted_iota(jnp.int32, spread.shape, 1) // rows
    return jnp.sum(jnp.where(tile == peer * SUBLANES, spread, 0.0), axis=0, keepdims=True).astype(jnp.int32)


def put_texts(packet_refs, text_ref):
    blocks = text_ref.shape[1] // LANES
    count = text_ref.shape[0] // len(packet_refs)
    pairs = []
    for i, ref in enumerate(packet_refs):
        rows = count // ref.shape[0]
        for k in range(blocks):
            block = ref[:, k * rows : (k + 1) * rows, :].reshape(count, LANES)
            text_ref[i * count : (i + 1) * count, k * LANES : (k + 1) * LANES] = block
        pairs.append(pairs_of(ref[:, blocks * rows :, :].reshape(-1, LANES), rows))
    return jnp.concatenate(pairs, axis=1)


def weight_kernel(first_ref, scalars_ref, own_ref, beside_ref, own_packet_ref, other_packet_ref, *refs):
    weights_ref, own_grad_ref, other_grad_ref, image_ref, text_ref, weight_ref, sem = refs
    half = own_ref.shape[0]
    image_ref[:half, :] = own_ref[...]
    image_ref[half:, :] = beside_ref[...]
    pairs = put_texts((own_packet_ref, other_packet_ref), text_ref)
    row = lax.broadcasted_iota(jnp.int32, (128, 1), 0)
    places = jnp.concatenate([row + first_ref[p] for p in range(2 * half // 128)], axis=0)
    images = image_ref[...]
    dots = lax.dot_general(images, text_ref[...], ROWS_BY_ROWS, preferred_element_type=jnp.float32)
    chance = 1.0 / (1.0 + jnp.exp2(dots * scalars_ref[1] + scalars_ref[2]))
    weight = (scalars_ref[0] * jnp.where(pairs == places, chance - 1.0, chance)).astype(jnp.bfloat16)
    weight_ref[...] = weight
    leaving = pltpu.make_async_copy(weight_ref, weights_ref, sem)
    leaving.start()
    grad = lax.dot_general(weight, images, COLUMNS_BY_ROWS, preferred_element_type=jnp.float32)
    count = own_grad_ref.shape[0]
    own_grad_ref[...] = grad[:count].astype(own_grad_ref.dtype)
    other_grad_ref[...] = grad[count:].astype(other_grad_ref.dtype)
    leaving.wait()


def weights_and_text_terms(first, scalars, own, beside, packets, other_packets, rows):
    half, width = own.shape
    count = packets.shape[0] * rows
    return pl.pallas_call(
        weight_kernel,
        in_specs=[smem, smem] + [vmem] * 4,
        out_specs=[hbm, vmem, vmem],
        out_shape=[
            jax.ShapeDtypeStruct((2 * half, 2 * count), jnp.bfloat16),
            jax.ShapeDtypeStruct((count, width), jnp.bfloat16),
            jax.ShapeDtypeStruct((count, width), jnp.bfloat16),
        ],
        scratch_shapes=[
            pltpu.VMEM((2 * half, width), jnp.bfloat16),
            pltpu.VMEM((2 * count, width), jnp.bfloat16),
            pltpu.VMEM((2 * half, 2 * count), jnp.bfloat16),
            pltpu.SemaphoreType.DMA,
        ],
        compiler_params=params(48),
        cost_estimate=pl.CostEstimate(
            flops=16 * half * count * width,
            bytes_accessed=4 * (half + count) * width + 8 * half * count,
            transcendentals=8 * half * count,
        ),
    )(first, scalars, own, beside, packets, other_packets)


def image_kernel(weight_ref, own_packet_ref, other_packet_ref, own_ref, beside_ref, text_ref):
    put_texts((own_packet_ref, other_packet_ref), text_ref)
    grad = jnp.dot(weight_ref[...], text_ref[...], preferred_element_type=jnp.float32)
    half = own_ref.shape[0]
    own_ref[...] = grad[:half].astype(own_ref.dtype)
    beside_ref[...] = grad[half:].astype(beside_ref.dtype)


def image_terms(weights, packets, other_packets, width):
    rows, count = weights.shape
    return pl.pallas_call(
        image_kernel,
        in_specs=[vmem] * 3,
        out_specs=[vmem] * 2,
        out_shape=[jax.ShapeDtypeStruct((rows // 2, width), jnp.bfloat16)] * 2,
        scratch_shapes=[pltpu.VMEM((count, width), jnp.bfloat16)],
        compiler_params=params(24),
        cost_estimate=pl.CostEstimate(
            flops=2 * rows * count * width, bytes_accessed=2 * (rows + count) * width + 2 * rows * count, transcendentals=0
        ),
    )(weights, packets, other_packets)


def backward_kernel(embed_ref, *refs):
    floats = embed_ref[...].astype(jnp.float32)
    inverse = inverse_norm(floats)
    unit = floats * inverse
    parts_refs, out_ref = refs[:-1], refs[-1]
    grad = None
    for ref in parts_refs:
        for part in [ref[...]] if len(ref.shape) == 2 else [ref[i] for i in range(ref.shape[0])]:
            part = part.astype(jnp.float32)
            grad = part if grad is None else grad + part
    along = jnp.sum(unit * grad, axis=-1, keepdims=True)
    out_ref[...] = ((grad - unit * along) * inverse).astype(out_ref.dtype)


def unit_backward(embed, *parts):
    return pl.pallas_call(
        backward_kernel,
        in_specs=[vmem] * (1 + len(parts)),
        out_specs=vmem,
        out_shape=jax.ShapeDtypeStruct(embed.shape, jnp.bfloat16),
        compiler_params=params(8),
    )(embed, *parts)


def shifted(array, axis, by):
    devices = lax.axis_size(axis)
    return lax.ppermute(array, axis, [(i, (i + by) % devices) for i in range(devices)])


def on_device(image_embed, text_embed, log_scale, logit_bias, pair_index):
    own_images, width = image_embed.shape
    own_texts = text_embed.shape[0]
    peers, ring = lax.axis_size(FAR), lax.axis_size("x")

    unit, packets = units_and_packets(pair_index, image_embed, text_embed, peers)
    packets = lax.all_to_all(packets, FAR, split_axis=0, concat_axis=0, tiled=True)
    own = lax.all_gather(unit, "x", axis=0, tiled=True)
    beside = shifted(own, "yl", 1)
    packets, beside = lax.optimization_barrier((packets, beside))
    other_packets = shifted(packets, "c", 1)

    scale = jnp.exp(log_scale)
    scalars = jnp.concatenate([scale, -math.log2(math.e) * scale, -math.log2(math.e) * logit_bias])
    far, yl, x, c = lax.axis_index(FAR), lax.axis_index("yl"), lax.axis_index("x"), lax.axis_index("c")
    first = jnp.stack(
        [(((far * 2 + half) * ring + place) * 2 + c) * own_images for half in (yl, 1 - yl) for place in range(ring)]
    ).astype(jnp.int32)
    weights, own_part, other_part = weights_and_text_terms(
        first, scalars, own, beside, packets, other_packets, own_texts
    )
    text_part = own_part.astype(jnp.float32) + shifted(other_part, "c", 1).astype(jnp.float32)
    text_parts = lax.all_to_all(
        text_part.astype(jnp.bfloat16).reshape(peers, own_texts, width), FAR, split_axis=0, concat_axis=0, tiled=True
    )

    own_part, beside_part = image_terms(weights, packets, other_packets, width)
    part = own_part.astype(jnp.float32) + shifted(beside_part, "yl", 1).astype(jnp.float32)
    part = part.astype(jnp.bfloat16).reshape(ring, own_images, width)
    parts = [lax.dynamic_index_in_dim(part, (x + s) % ring, 0, keepdims=False) for s in range(ring)]
    parts = parts[:1] + [shifted(parts[s], "x", s) for s in range(1, ring)]
    return unit_backward(image_embed, *parts), unit_backward(text_embed, text_parts)


def solution(mesh):
    split = Mesh(mesh.devices.reshape(SIZES), AXES)
    rows = P(AXES, None)
    return jax.shard_map(
        on_device,
        mesh=split,
        in_specs=(rows, rows, P(), P(), P(AXES)),
        out_specs=(rows, rows),
        check_vma=False,
    )
```

```python
import math

import jax
import jax.numpy as jnp
from jax import lax
from jax.experimental import pallas as pl
from jax.experimental.pallas import tpu as pltpu
from jax.sharding import Mesh
from jax.sharding import PartitionSpec as P

AXES = ("z", "y", "x", "c")
SIZES = (8, 8, 4, 2)
LANES = 128
PIECES = 4
MIB = 1024 * 1024
ROWS_BY_ROWS = (((1,), (1,)), ((), ()))
COLUMNS_BY_ROWS = (((0,), (0,)), ((), ()))

smem = pl.BlockSpec(memory_space=pltpu.SMEM)
vmem = pl.BlockSpec(memory_space=pltpu.VMEM)
hbm = pl.BlockSpec(memory_space=pltpu.HBM)


def params(mib):
    return pltpu.CompilerParams(vmem_limit_bytes=mib * MIB)


def inverse_norm(floats):
    return lax.rsqrt(jnp.sum(floats * floats, axis=-1, keepdims=True) + 1e-06)


def unit_kernel(embed_ref, unit_ref):
    floats = embed_ref[...].astype(jnp.float32)
    unit_ref[...] = (floats * inverse_norm(floats)).astype(unit_ref.dtype)


def units(embed):
    return pl.pallas_call(
        unit_kernel,
        in_specs=[vmem],
        out_specs=vmem,
        out_shape=jax.ShapeDtypeStruct(embed.shape, jnp.bfloat16),
        compiler_params=params(56),
    )(embed)


def packet_kernel(pair_ref, text_ref, packet_ref):
    rows, width = text_ref.shape
    floats = text_ref[...].astype(jnp.float32)
    unit = (floats * inverse_norm(floats)).astype(packet_ref.dtype)
    row = lax.broadcasted_iota(jnp.int32, (rows, LANES), 0)
    lane = lax.broadcasted_iota(jnp.int32, (rows, LANES), 1)
    index = jnp.zeros((rows, LANES), jnp.int32)
    for i in range(rows):
        index = jnp.where(row == i, pair_ref[i], index)
    digits = jnp.where(lane == 0, index >> 8, jnp.where(lane == 1, index & 255, 0))
    digits = digits.astype(jnp.float32).astype(packet_ref.dtype)
    for peer in range(packet_ref.shape[0]):
        packet_ref[peer, :, :width] = unit
        packet_ref[peer, :, width:] = digits


def text_packets(pair_index, embed, peers):
    rows, width = embed.shape
    return pl.pallas_call(
        packet_kernel,
        in_specs=[smem, vmem],
        out_specs=vmem,
        out_shape=jax.ShapeDtypeStruct((peers, rows, width + LANES), jnp.bfloat16),
        compiler_params=params(56),
    )(pair_index, embed)


def copies_of(source_ref, target_ref, sems, first):
    size = target_ref.shape[0] // PIECES
    pieces = [pl.ds(i * size, size) for i in range(PIECES)]
    return [pltpu.make_async_copy(source_ref.at[p], target_ref.at[p], sems.at[first + i]) for i, p in enumerate(pieces)]


def weight_kernel(first_ref, scalars_ref, images_ref, own_ref, other_ref, *refs):
    weights_ref, grads_ref, image_ref, text_ref, weight_ref, grad_ref, sems = refs
    arriving = copies_of(images_ref, image_ref, sems, 0)
    for copy in arriving:
        copy.start()
    height, width = image_ref.shape
    count = own_ref.shape[0]
    text_ref[:count, :] = own_ref[...]
    text_ref[count:, :] = other_ref[...]
    digits = text_ref[:, width:].astype(jnp.float32).T
    pairs = (digits[0:1] * 256.0 + digits[1:2]).astype(jnp.int32)
    row = lax.broadcasted_iota(jnp.int32, (128, 1), 0)
    texts = text_ref[:, :width]
    half = height // 2
    weights = copies_of(weight_ref, weights_ref, sems, PIECES)
    grads = copies_of(grad_ref, grads_ref, sems, 2 * PIECES)
    pieces = PIECES // 2
    for i in range(2):
        for copy in arriving[i * pieces : (i + 1) * pieces]:
            copy.wait()
        images = image_ref[i * half : (i + 1) * half, :]
        rows = jnp.concatenate([row + first_ref[i * half // 128 + p] for p in range(half // 128)], axis=0)
        dots = lax.dot_general(images, texts, ROWS_BY_ROWS, preferred_element_type=jnp.float32)
        chance = 1.0 / (1.0 + jnp.exp2(dots * scalars_ref[1] + scalars_ref[2]))
        weight = (scalars_ref[0] * jnp.where(pairs == rows, chance - 1.0, chance)).astype(jnp.bfloat16)
        weight_ref[i * half : (i + 1) * half, :] = weight
        for copy in weights[i * pieces : (i + 1) * pieces]:
            copy.start()
        grad = jnp.dot(weight, texts, preferred_element_type=jnp.float32)
        grad_ref[i * half : (i + 1) * half, :] = grad.astype(grad_ref.dtype)
        for copy in grads[i * pieces : (i + 1) * pieces]:
            copy.start()
    for copy in weights + grads:
        copy.wait()


def weights_and_image_terms(first, scalars, images, own, other):
    rows, width = images.shape
    count, wide = own.shape
    texts = 2 * count
    return pl.pallas_call(
        weight_kernel,
        in_specs=[smem, smem, hbm, vmem, vmem],
        out_specs=[hbm, hbm],
        out_shape=[
            jax.ShapeDtypeStruct((rows, texts), jnp.bfloat16),
            jax.ShapeDtypeStruct((rows, width), jnp.bfloat16),
        ],
        scratch_shapes=[
            pltpu.VMEM((rows, width), jnp.bfloat16),
            pltpu.VMEM((texts, wide), jnp.bfloat16),
            pltpu.VMEM((rows, texts), jnp.bfloat16),
            pltpu.VMEM((rows, width), jnp.bfloat16),
            pltpu.SemaphoreType.DMA((3 * PIECES,)),
        ],
        compiler_params=params(51),
        cost_estimate=pl.CostEstimate(
            flops=4 * rows * texts * width, bytes_accessed=4 * (rows + texts) * width, transcendentals=2 * rows * texts
        ),
    )(first, scalars, images, own, other)


def text_kernel(weights_ref, images_ref, own_grad_ref, other_grad_ref, weight_ref, image_ref, sems):
    arriving = copies_of(weights_ref, weight_ref, sems, 0) + copies_of(images_ref, image_ref, sems, PIECES)
    for copy in arriving:
        copy.start()
    for copy in arriving:
        copy.wait()
    count = own_grad_ref.shape[0]
    grad = lax.dot_general(weight_ref[...], image_ref[...], COLUMNS_BY_ROWS, preferred_element_type=jnp.float32)
    own_grad_ref[...] = grad[:count].astype(own_grad_ref.dtype)
    other_grad_ref[...] = grad[count:].astype(other_grad_ref.dtype)


def text_terms(weights, images):
    rows, texts = weights.shape
    width = images.shape[1]
    return pl.pallas_call(
        text_kernel,
        in_specs=[hbm] * 2,
        out_specs=[vmem] * 2,
        out_shape=[jax.ShapeDtypeStruct((texts // 2, width), jnp.bfloat16)] * 2,
        scratch_shapes=[
            pltpu.VMEM(weights.shape, jnp.bfloat16),
            pltpu.VMEM(images.shape, jnp.bfloat16),
            pltpu.SemaphoreType.DMA((2 * PIECES,)),
        ],
        compiler_params=params(58),
        cost_estimate=pl.CostEstimate(
            flops=2 * rows * texts * width, bytes_accessed=2 * (rows + texts) * width, transcendentals=0
        ),
    )(weights, images)


def project(embed_ref, grad, out_ref):
    floats = embed_ref[...].astype(jnp.float32)
    inverse = inverse_norm(floats)
    unit = floats * inverse
    along = jnp.sum(unit * grad, axis=-1, keepdims=True)
    out_ref[...] = ((grad - unit * along) * inverse).astype(out_ref.dtype)


def backward_kernel(image_ref, text_ref, image_grad_ref, text_grads_ref, image_out_ref, text_out_ref):
    project(image_ref, image_grad_ref[...].astype(jnp.float32), image_out_ref)
    text_grad = text_grads_ref[0].astype(jnp.float32)
    for part in range(1, text_grads_ref.shape[0]):
        text_grad += text_grads_ref[part].astype(jnp.float32)
    project(text_ref, text_grad, text_out_ref)


def unit_backward(image_embed, text_embed, image_grad, text_grads):
    return pl.pallas_call(
        backward_kernel,
        in_specs=[vmem] * 4,
        out_specs=[vmem] * 2,
        out_shape=[
            jax.ShapeDtypeStruct(image_embed.shape, jnp.bfloat16),
            jax.ShapeDtypeStruct(text_embed.shape, jnp.bfloat16),
        ],
        compiler_params=params(8),
    )(image_embed, text_embed, image_grad, text_grads)


def image_rings():
    depth, length, width, cores = SIZES
    rings = []
    for z in range(depth):
        for x in range(width):
            for c in range(cores):
                ring = [((z * length + y) * width + x) * cores + c for y in range(length)]
                rings.append(ring if c == 0 else ring[::-1])
    return rings


def exchanged(array):
    return lax.ppermute(array, "c", [(0, 1), (1, 0)])


def spread(copies, axis):
    return lax.all_to_all(copies, axis, split_axis=0, concat_axis=0, tiled=True).reshape(-1, copies.shape[2])


def parted(rows, axis):
    parts = rows.reshape(lax.axis_size(axis), -1, rows.shape[1])
    return lax.all_to_all(parts, axis, split_axis=0, concat_axis=0, tiled=True)


def on_device(image_embed, text_embed, log_scale, logit_bias, pair_index):
    own_images = image_embed.shape[0]
    rings = image_rings()
    images = lax.all_gather(units(image_embed), AXES, axis=0, tiled=True, axis_index_groups=rings)

    texts = spread(text_packets(pair_index, text_embed, lax.axis_size("z")), "z")
    own = spread(jnp.broadcast_to(texts[None], (lax.axis_size("x"),) + texts.shape), "x")
    other = exchanged(own)

    scale = jnp.exp(log_scale)
    scalars = jnp.concatenate([scale, -math.log2(math.e) * scale, -math.log2(math.e) * logit_bias])
    z, x, c = lax.axis_index("z"), lax.axis_index("x"), lax.axis_index("c")
    place = jnp.arange(SIZES[1], dtype=jnp.int32)
    place = jnp.where(c == 0, place, SIZES[1] - 1 - place)
    first = (((z * SIZES[1] + place) * SIZES[2] + x) * SIZES[3] + c) * own_images

    weights, image_part = weights_and_image_terms(first.astype(jnp.int32), scalars, images, own, other)
    image_grad = lax.psum_scatter(image_part, AXES, scatter_dimension=0, tiled=True, axis_index_groups=rings)

    own_part, other_part = text_terms(weights, images)
    text_part = own_part.astype(jnp.float32) + exchanged(other_part).astype(jnp.float32)
    text_part = jnp.sum(parted(text_part.astype(jnp.bfloat16), "x").astype(jnp.float32), axis=0)
    text_grads = parted(text_part.astype(jnp.bfloat16), "z")
    return unit_backward(image_embed, text_embed, image_grad, text_grads)


def solution(mesh):
    split = Mesh(mesh.devices.reshape(SIZES), AXES)
    rows = P(AXES, None)
    return jax.shard_map(
        on_device,
        mesh=split,
        in_specs=(rows, rows, P(), P(), P(AXES)),
        out_specs=(rows, rows),
        check_vma=False,
    )
```

```python
import math

import jax
import jax.numpy as jnp
from jax import lax
from jax.experimental import pallas as pl
from jax.experimental.pallas import tpu as pltpu
from jax.sharding import Mesh
from jax.sharding import PartitionSpec as P

AXES = ("z", "y", "x", "c")
SIZES = (8, 8, 4, 2)
LANES = 128
PIECES = 4
MIB = 1024 * 1024
ROWS_BY_ROWS = (((1,), (1,)), ((), ()))
COLUMNS_BY_ROWS = (((0,), (0,)), ((), ()))

smem = pl.BlockSpec(memory_space=pltpu.SMEM)
vmem = pl.BlockSpec(memory_space=pltpu.VMEM)
hbm = pl.BlockSpec(memory_space=pltpu.HBM)


def params(mib):
    return pltpu.CompilerParams(vmem_limit_bytes=mib * MIB)


def inverse_norm(floats):
    return lax.rsqrt(jnp.sum(floats * floats, axis=-1, keepdims=True) + 1e-06)


def unit_kernel(embed_ref, unit_ref):
    floats = embed_ref[...].astype(jnp.float32)
    unit_ref[...] = (floats * inverse_norm(floats)).astype(unit_ref.dtype)


def units(embed):
    return pl.pallas_call(
        unit_kernel,
        in_specs=[vmem],
        out_specs=vmem,
        out_shape=jax.ShapeDtypeStruct(embed.shape, jnp.bfloat16),
        compiler_params=params(56),
    )(embed)


def packet_kernel(pair_ref, text_ref, packet_ref):
    rows, width = text_ref.shape
    floats = text_ref[...].astype(jnp.float32)
    unit = (floats * inverse_norm(floats)).astype(packet_ref.dtype)
    row = lax.broadcasted_iota(jnp.int32, (rows, LANES), 0)
    lane = lax.broadcasted_iota(jnp.int32, (rows, LANES), 1)
    index = jnp.zeros((rows, LANES), jnp.int32)
    for i in range(rows):
        index = jnp.where(row == i, pair_ref[i], index)
    digits = jnp.where(lane == 0, index >> 8, jnp.where(lane == 1, index & 255, 0))
    digits = digits.astype(jnp.float32).astype(packet_ref.dtype)
    for peer in range(packet_ref.shape[0]):
        packet_ref[peer, :, :width] = unit
        packet_ref[peer, :, width:] = digits


def text_packets(pair_index, embed, peers):
    rows, width = embed.shape
    return pl.pallas_call(
        packet_kernel,
        in_specs=[smem, vmem],
        out_specs=vmem,
        out_shape=jax.ShapeDtypeStruct((peers, rows, width + LANES), jnp.bfloat16),
        compiler_params=params(56),
    )(pair_index, embed)


def copies_of(source_ref, target_ref, sems, first):
    size = target_ref.shape[0] // PIECES
    pieces = [pl.ds(i * size, size) for i in range(PIECES)]
    return [pltpu.make_async_copy(source_ref.at[p], target_ref.at[p], sems.at[first + i]) for i, p in enumerate(pieces)]


def pair_kernel(first_ref, scalars_ref, images_ref, own_ref, other_ref, *refs):
    image_grads_ref, own_grad_ref, other_grad_ref, image_ref, text_ref, grad_ref, sems = refs
    arriving = copies_of(images_ref, image_ref, sems, 0)
    for copy in arriving:
        copy.start()
    leaving = copies_of(grad_ref, image_grads_ref, sems, PIECES)
    height, width = image_ref.shape
    count = own_ref.shape[0]
    text_ref[:count, :] = own_ref[...]
    text_ref[count:, :] = other_ref[...]
    digits = text_ref[:, width:].astype(jnp.float32).T
    pairs = (digits[0:1] * 256.0 + digits[1:2]).astype(jnp.int32)
    row = lax.broadcasted_iota(jnp.int32, (128, 1), 0)
    texts = text_ref[:, :width]
    half, pieces = height // 2, PIECES // 2
    weights = []
    for i in range(2):
        for copy in arriving[i * pieces : (i + 1) * pieces]:
            copy.wait()
        images = image_ref[i * half : (i + 1) * half, :]
        rows = jnp.concatenate([row + first_ref[i * half // 128 + p] for p in range(half // 128)], axis=0)
        dots = lax.dot_general(images, texts, ROWS_BY_ROWS, preferred_element_type=jnp.float32)
        chance = 1.0 / (1.0 + jnp.exp2(dots * scalars_ref[1] + scalars_ref[2]))
        weights.append((scalars_ref[0] * jnp.where(pairs == rows, chance - 1.0, chance)).astype(jnp.bfloat16))
        grad = jnp.dot(weights[i], texts, preferred_element_type=jnp.float32)
        grad_ref[i * half : (i + 1) * half, :] = grad.astype(grad_ref.dtype)
        for copy in leaving[i * pieces : (i + 1) * pieces]:
            copy.start()
    weight = jnp.concatenate(weights, axis=0)
    text_grad = lax.dot_general(weight, image_ref[...], COLUMNS_BY_ROWS, preferred_element_type=jnp.float32)
    own_grad_ref[...] = text_grad[:count].astype(own_grad_ref.dtype)
    other_grad_ref[...] = text_grad[count:].astype(other_grad_ref.dtype)
    for copy in leaving:
        copy.wait()


def pair_terms(first, scalars, images, own, other):
    rows, width = images.shape
    count, wide = own.shape
    texts = 2 * count
    return pl.pallas_call(
        pair_kernel,
        in_specs=[smem, smem, hbm, vmem, vmem],
        out_specs=[hbm, vmem, vmem],
        out_shape=[
            jax.ShapeDtypeStruct((rows, width), jnp.bfloat16),
            jax.ShapeDtypeStruct((count, width), jnp.bfloat16),
            jax.ShapeDtypeStruct((count, width), jnp.bfloat16),
        ],
        scratch_shapes=[
            pltpu.VMEM((rows, width), jnp.bfloat16),
            pltpu.VMEM((texts, wide), jnp.bfloat16),
            pltpu.VMEM((rows, width), jnp.bfloat16),
            pltpu.SemaphoreType.DMA((2 * PIECES,)),
        ],
        compiler_params=params(48),
        cost_estimate=pl.CostEstimate(
            flops=6 * rows * texts * width, bytes_accessed=4 * (rows + texts) * width, transcendentals=2 * rows * texts
        ),
    )(first, scalars, images, own, other)


def project(embed_ref, grad, out_ref):
    floats = embed_ref[...].astype(jnp.float32)
    inverse = inverse_norm(floats)
    unit = floats * inverse
    along = jnp.sum(unit * grad, axis=-1, keepdims=True)
    out_ref[...] = ((grad - unit * along) * inverse).astype(out_ref.dtype)


def backward_kernel(image_ref, text_ref, image_grad_ref, text_grads_ref, image_out_ref, text_out_ref):
    project(image_ref, image_grad_ref[...].astype(jnp.float32), image_out_ref)
    text_grad = text_grads_ref[0].astype(jnp.float32)
    for part in range(1, text_grads_ref.shape[0]):
        text_grad += text_grads_ref[part].astype(jnp.float32)
    project(text_ref, text_grad, text_out_ref)


def unit_backward(image_embed, text_embed, image_grad, text_grads):
    return pl.pallas_call(
        backward_kernel,
        in_specs=[vmem] * 4,
        out_specs=[vmem] * 2,
        out_shape=[
            jax.ShapeDtypeStruct(image_embed.shape, jnp.bfloat16),
            jax.ShapeDtypeStruct(text_embed.shape, jnp.bfloat16),
        ],
        compiler_params=params(8),
    )(image_embed, text_embed, image_grad, text_grads)


def image_rings():
    depth, length, width, cores = SIZES
    rings = []
    for z in range(depth):
        for x in range(width):
            for c in range(cores):
                ring = [((z * length + y) * width + x) * cores + c for y in range(length)]
                rings.append(ring if c == 0 else ring[::-1])
    return rings


def exchanged(array):
    return lax.ppermute(array, "c", [(0, 1), (1, 0)])


def spread(copies, axis):
    return lax.all_to_all(copies, axis, split_axis=0, concat_axis=0, tiled=True).reshape(-1, copies.shape[2])


def parted(rows, axis):
    parts = rows.reshape(lax.axis_size(axis), -1, rows.shape[1])
    return lax.all_to_all(parts, axis, split_axis=0, concat_axis=0, tiled=True)


def on_device(image_embed, text_embed, log_scale, logit_bias, pair_index):
    own_images = image_embed.shape[0]
    rings = image_rings()
    images = lax.all_gather(units(image_embed), AXES, axis=0, tiled=True, axis_index_groups=rings)

    texts = spread(text_packets(pair_index, text_embed, lax.axis_size("z")), "z")
    own = spread(jnp.broadcast_to(texts[None], (lax.axis_size("x"),) + texts.shape), "x")
    other = exchanged(own)

    scale = jnp.exp(log_scale)
    scalars = jnp.concatenate([scale, -math.log2(math.e) * scale, -math.log2(math.e) * logit_bias])
    z, x, c = lax.axis_index("z"), lax.axis_index("x"), lax.axis_index("c")
    place = jnp.arange(SIZES[1], dtype=jnp.int32)
    place = jnp.where(c == 0, place, SIZES[1] - 1 - place)
    first = (((z * SIZES[1] + place) * SIZES[2] + x) * SIZES[3] + c) * own_images

    image_part, own_part, other_part = pair_terms(first.astype(jnp.int32), scalars, images, own, other)
    image_grad = lax.psum_scatter(image_part, AXES, scatter_dimension=0, tiled=True, axis_index_groups=rings)

    text_part = own_part.astype(jnp.float32) + exchanged(other_part).astype(jnp.float32)
    text_part = jnp.sum(parted(text_part.astype(jnp.bfloat16), "x").astype(jnp.float32), axis=0)
    text_grads = parted(text_part.astype(jnp.bfloat16), "z")
    return unit_backward(image_embed, text_embed, image_grad, text_grads)


def solution(mesh):
    split = Mesh(mesh.devices.reshape(SIZES), AXES)
    rows = P(AXES, None)
    return jax.shard_map(
        on_device,
        mesh=split,
        in_specs=(rows, rows, P(), P(), P(AXES)),
        out_specs=(rows, rows),
        check_vma=False,
    )
```

```python
import math

import jax
import jax.numpy as jnp
from jax import lax
from jax.experimental import pallas as pl
from jax.experimental.pallas import tpu as pltpu
from jax.sharding import Mesh
from jax.sharding import PartitionSpec as P

AXES = ("z", "y", "x", "c")
SIZES = (8, 8, 4, 2)
LANES = 128
MIB = 1024 * 1024
ROWS_BY_ROWS = (((1,), (1,)), ((), ()))
COLUMNS_BY_ROWS = (((0,), (0,)), ((), ()))

smem = pl.BlockSpec(memory_space=pltpu.SMEM)
vmem = pl.BlockSpec(memory_space=pltpu.VMEM)


def params(mib):
    return pltpu.CompilerParams(vmem_limit_bytes=mib * MIB)


def inverse_norm(floats):
    return lax.rsqrt(jnp.sum(floats * floats, axis=-1, keepdims=True) + 1e-06)


def unit_kernel(embed_ref, unit_ref):
    floats = embed_ref[...].astype(jnp.float32)
    unit_ref[...] = (floats * inverse_norm(floats)).astype(unit_ref.dtype)


def units(embed):
    return pl.pallas_call(
        unit_kernel,
        in_specs=[vmem],
        out_specs=vmem,
        out_shape=jax.ShapeDtypeStruct(embed.shape, jnp.bfloat16),
        compiler_params=params(56),
    )(embed)


def packet_kernel(pair_ref, text_ref, packet_ref):
    rows, width = text_ref.shape
    floats = text_ref[...].astype(jnp.float32)
    unit = (floats * inverse_norm(floats)).astype(packet_ref.dtype)
    row = lax.broadcasted_iota(jnp.int32, (rows, LANES), 0)
    lane = lax.broadcasted_iota(jnp.int32, (rows, LANES), 1)
    index = jnp.zeros((rows, LANES), jnp.int32)
    for i in range(rows):
        index = jnp.where(row == i, pair_ref[i], index)
    digits = jnp.where(lane == 0, index >> 8, jnp.where(lane == 1, index & 255, 0))
    digits = digits.astype(jnp.float32).astype(packet_ref.dtype)
    for peer in range(packet_ref.shape[0]):
        packet_ref[peer, :, :width] = unit
        packet_ref[peer, :, width:] = digits


def text_packets(pair_index, embed, peers):
    rows, width = embed.shape
    return pl.pallas_call(
        packet_kernel,
        in_specs=[smem, vmem],
        out_specs=vmem,
        out_shape=jax.ShapeDtypeStruct((peers, rows, width + LANES), jnp.bfloat16),
        compiler_params=params(56),
    )(pair_index, embed)


def pair_kernel(first_ref, scalars_ref, image_ref, own_ref, other_ref, *refs):
    image_grad_ref, own_grad_ref, other_grad_ref, text_ref = refs
    width = image_ref.shape[1]
    count = own_ref.shape[0]
    text_ref[:count, :] = own_ref[...]
    text_ref[count:, :] = other_ref[...]
    digits = text_ref[:, width:].astype(jnp.float32).T
    pairs = (digits[0:1] * 256.0 + digits[1:2]).astype(jnp.int32)
    row = lax.broadcasted_iota(jnp.int32, (128, 1), 0)
    rows = jnp.concatenate([row + first_ref[p] for p in range(image_ref.shape[0] // 128)], axis=0)
    texts = text_ref[:, :width]
    images = image_ref[...]
    dots = lax.dot_general(images, texts, ROWS_BY_ROWS, preferred_element_type=jnp.float32)
    chance = 1.0 / (1.0 + jnp.exp2(dots * scalars_ref[1] + scalars_ref[2]))
    weight = (scalars_ref[0] * jnp.where(pairs == rows, chance - 1.0, chance)).astype(jnp.bfloat16)
    image_grad_ref[...] = jnp.dot(weight, texts, preferred_element_type=jnp.float32).astype(image_grad_ref.dtype)
    text_grad = lax.dot_general(weight, images, COLUMNS_BY_ROWS, preferred_element_type=jnp.float32)
    own_grad_ref[...] = text_grad[:count].astype(own_grad_ref.dtype)
    other_grad_ref[...] = text_grad[count:].astype(other_grad_ref.dtype)


def pair_terms(first, scalars, images, own, other):
    rows, width = images.shape
    count, wide = own.shape
    texts = 2 * count
    return pl.pallas_call(
        pair_kernel,
        in_specs=[smem, smem, vmem, vmem, vmem],
        out_specs=[vmem] * 3,
        out_shape=[
            jax.ShapeDtypeStruct((rows, width), jnp.bfloat16),
            jax.ShapeDtypeStruct((count, width), jnp.bfloat16),
            jax.ShapeDtypeStruct((count, width), jnp.bfloat16),
        ],
        scratch_shapes=[pltpu.VMEM((texts, wide), jnp.bfloat16)],
        compiler_params=params(32),
        cost_estimate=pl.CostEstimate(
            flops=6 * rows * texts * width, bytes_accessed=4 * (rows + texts) * width, transcendentals=2 * rows * texts
        ),
    )(first, scalars, images, own, other)


def project(embed_ref, grad, out_ref):
    floats = embed_ref[...].astype(jnp.float32)
    inverse = inverse_norm(floats)
    unit = floats * inverse
    along = jnp.sum(unit * grad, axis=-1, keepdims=True)
    out_ref[...] = ((grad - unit * along) * inverse).astype(out_ref.dtype)


def backward_kernel(image_ref, text_ref, image_grad_ref, text_grads_ref, image_out_ref, text_out_ref):
    project(image_ref, image_grad_ref[...].astype(jnp.float32), image_out_ref)
    text_grad = text_grads_ref[0].astype(jnp.float32)
    for part in range(1, text_grads_ref.shape[0]):
        text_grad += text_grads_ref[part].astype(jnp.float32)
    project(text_ref, text_grad, text_out_ref)


def unit_backward(image_embed, text_embed, image_grad, text_grads):
    return pl.pallas_call(
        backward_kernel,
        in_specs=[vmem] * 4,
        out_specs=[vmem] * 2,
        out_shape=[
            jax.ShapeDtypeStruct(image_embed.shape, jnp.bfloat16),
            jax.ShapeDtypeStruct(text_embed.shape, jnp.bfloat16),
        ],
        compiler_params=params(58),
    )(image_embed, text_embed, image_grad, text_grads)


def image_rings():
    depth, length, width, cores = SIZES
    rings = []
    for z in range(depth):
        for x in range(width):
            for c in range(cores):
                ring = [((z * length + y) * width + x) * cores + c for y in range(length)]
                rings.append(ring if c == 0 else ring[::-1])
    return rings


def exchanged(array):
    return lax.ppermute(array, "c", [(0, 1), (1, 0)])


def spread(copies, axis):
    return lax.all_to_all(copies, axis, split_axis=0, concat_axis=0, tiled=True).reshape(-1, copies.shape[2])


def parted(rows, axis):
    parts = rows.reshape(lax.axis_size(axis), -1, rows.shape[1])
    return lax.all_to_all(parts, axis, split_axis=0, concat_axis=0, tiled=True)


def on_device(image_embed, text_embed, log_scale, logit_bias, pair_index):
    own_images = image_embed.shape[0]
    rings = image_rings()
    images = lax.all_gather(units(image_embed), AXES, axis=0, tiled=True, axis_index_groups=rings)

    texts = spread(text_packets(pair_index, text_embed, lax.axis_size("z")), "z")
    own = spread(jnp.broadcast_to(texts[None], (lax.axis_size("x"),) + texts.shape), "x")
    other = exchanged(own)

    scale = jnp.exp(log_scale)
    scalars = jnp.concatenate([scale, -math.log2(math.e) * scale, -math.log2(math.e) * logit_bias])
    z, x, c = lax.axis_index("z"), lax.axis_index("x"), lax.axis_index("c")
    place = jnp.arange(SIZES[1], dtype=jnp.int32)
    place = jnp.where(c == 0, place, SIZES[1] - 1 - place)
    first = (((z * SIZES[1] + place) * SIZES[2] + x) * SIZES[3] + c) * own_images

    image_part, own_part, other_part = pair_terms(first.astype(jnp.int32), scalars, images, own, other)
    image_grad = lax.psum_scatter(image_part, AXES, scatter_dimension=0, tiled=True, axis_index_groups=rings)

    text_part = own_part.astype(jnp.float32) + exchanged(other_part).astype(jnp.float32)
    text_part = jnp.sum(parted(text_part.astype(jnp.bfloat16), "x").astype(jnp.float32), axis=0)
    text_grads = parted(text_part.astype(jnp.bfloat16), "z")
    return unit_backward(image_embed, text_embed, image_grad, text_grads)


def solution(mesh):
    split = Mesh(mesh.devices.reshape(SIZES), AXES)
    rows = P(AXES, None)
    return jax.shard_map(
        on_device,
        mesh=split,
        in_specs=(rows, rows, P(), P(), P(AXES)),
        out_specs=(rows, rows),
        check_vma=False,
    )
```

```python
import math

import jax
import jax.numpy as jnp
from jax import lax
from jax.experimental import pallas as pl
from jax.experimental.pallas import tpu as pltpu
from jax.sharding import Mesh
from jax.sharding import PartitionSpec as P

AXES = ("z", "y", "x", "c")
SIZES = (8, 8, 4, 2)
LANES = 128
MIB = 1024 * 1024
ROWS_BY_ROWS = (((1,), (1,)), ((), ()))
COLUMNS_BY_ROWS = (((0,), (0,)), ((), ()))

smem = pl.BlockSpec(memory_space=pltpu.SMEM)
vmem = pl.BlockSpec(memory_space=pltpu.VMEM)


def params(mib):
    return pltpu.CompilerParams(vmem_limit_bytes=mib * MIB)


def inverse_norm(floats):
    return lax.rsqrt(jnp.sum(floats * floats, axis=-1, keepdims=True) + 1e-06)


def packet_kernel(pair_ref, text_ref, packet_ref):
    rows, width = text_ref.shape
    floats = text_ref[...].astype(jnp.float32)
    unit = (floats * inverse_norm(floats)).astype(packet_ref.dtype)
    row = lax.broadcasted_iota(jnp.int32, (rows, LANES), 0)
    lane = lax.broadcasted_iota(jnp.int32, (rows, LANES), 1)
    index = jnp.zeros((rows, LANES), jnp.int32)
    for i in range(rows):
        index = jnp.where(row == i, pair_ref[i], index)
    digits = jnp.where(lane == 0, index >> 8, jnp.where(lane == 1, index & 255, 0))
    digits = digits.astype(jnp.float32).astype(packet_ref.dtype)
    for peer in range(packet_ref.shape[0]):
        packet_ref[peer, :, :width] = unit
        packet_ref[peer, :, width:] = digits


def text_packets(pair_index, embed, peers):
    rows, width = embed.shape
    return pl.pallas_call(
        packet_kernel,
        in_specs=[smem, vmem],
        out_specs=vmem,
        out_shape=jax.ShapeDtypeStruct((peers, rows, width + LANES), jnp.bfloat16),
        compiler_params=params(56),
    )(pair_index, embed)


def pair_kernel(first_ref, scalars_ref, image_ref, own_ref, other_ref, *refs):
    image_grad_ref, own_grad_ref, other_grad_ref, text_ref = refs
    width = image_ref.shape[1]
    count = own_ref.shape[0]
    text_ref[:count, :] = own_ref[...]
    text_ref[count:, :] = other_ref[...]
    digits = text_ref[:, width:].astype(jnp.float32).T
    pairs = (digits[0:1] * 256.0 + digits[1:2]).astype(jnp.int32)
    row = lax.broadcasted_iota(jnp.int32, (128, 1), 0)
    rows = jnp.concatenate([row + first_ref[p] for p in range(image_ref.shape[0] // 128)], axis=0)
    texts = text_ref[:, :width]
    images = image_ref[...]
    inverse = inverse_norm(images.astype(jnp.float32))
    dots = lax.dot_general(images, texts, ROWS_BY_ROWS, preferred_element_type=jnp.float32)
    chance = 1.0 / (1.0 + jnp.exp2(dots * (inverse * scalars_ref[1]) + scalars_ref[2]))
    floats = scalars_ref[0] * jnp.where(pairs == rows, chance - 1.0, chance)
    weight = floats.astype(jnp.bfloat16)
    scaled = (floats * inverse).astype(jnp.bfloat16)
    image_grad_ref[...] = jnp.dot(weight, texts, preferred_element_type=jnp.float32).astype(image_grad_ref.dtype)
    text_grad = lax.dot_general(scaled, images, COLUMNS_BY_ROWS, preferred_element_type=jnp.float32)
    own_grad_ref[...] = text_grad[:count].astype(own_grad_ref.dtype)
    other_grad_ref[...] = text_grad[count:].astype(other_grad_ref.dtype)


def pair_terms(first, scalars, images, own, other):
    rows, width = images.shape
    count, wide = own.shape
    texts = 2 * count
    return pl.pallas_call(
        pair_kernel,
        in_specs=[smem, smem, vmem, vmem, vmem],
        out_specs=[vmem] * 3,
        out_shape=[
            jax.ShapeDtypeStruct((rows, width), jnp.bfloat16),
            jax.ShapeDtypeStruct((count, width), jnp.bfloat16),
            jax.ShapeDtypeStruct((count, width), jnp.bfloat16),
        ],
        scratch_shapes=[pltpu.VMEM((texts, wide), jnp.bfloat16)],
        compiler_params=params(32),
        cost_estimate=pl.CostEstimate(
            flops=6 * rows * texts * width, bytes_accessed=4 * (rows + texts) * width, transcendentals=2 * rows * texts
        ),
    )(first, scalars, images, own, other)


def project(embed_ref, grad, out_ref):
    floats = embed_ref[...].astype(jnp.float32)
    inverse = inverse_norm(floats)
    unit = floats * inverse
    along = jnp.sum(unit * grad, axis=-1, keepdims=True)
    out_ref[...] = ((grad - unit * along) * inverse).astype(out_ref.dtype)


def backward_kernel(image_ref, text_ref, image_grad_ref, text_grads_ref, image_out_ref, text_out_ref):
    project(image_ref, image_grad_ref[...].astype(jnp.float32), image_out_ref)
    text_grad = text_grads_ref[0].astype(jnp.float32)
    for part in range(1, text_grads_ref.shape[0]):
        text_grad += text_grads_ref[part].astype(jnp.float32)
    project(text_ref, text_grad, text_out_ref)


def unit_backward(image_embed, text_embed, image_grad, text_grads):
    return pl.pallas_call(
        backward_kernel,
        in_specs=[vmem] * 4,
        out_specs=[vmem] * 2,
        out_shape=[
            jax.ShapeDtypeStruct(image_embed.shape, jnp.bfloat16),
            jax.ShapeDtypeStruct(text_embed.shape, jnp.bfloat16),
        ],
        compiler_params=params(8),
    )(image_embed, text_embed, image_grad, text_grads)


def image_rings():
    depth, length, width, cores = SIZES
    rings = []
    for z in range(depth):
        for x in range(width):
            for c in range(cores):
                ring = [((z * length + y) * width + x) * cores + c for y in range(length)]
                rings.append(ring if c == 0 else ring[::-1])
    return rings


def exchanged(array):
    return lax.ppermute(array, "c", [(0, 1), (1, 0)])


def spread(copies, axis):
    return lax.all_to_all(copies, axis, split_axis=0, concat_axis=0, tiled=True).reshape(-1, copies.shape[2])


def parted(rows, axis):
    parts = rows.reshape(lax.axis_size(axis), -1, rows.shape[1])
    return lax.all_to_all(parts, axis, split_axis=0, concat_axis=0, tiled=True)


def on_device(image_embed, text_embed, log_scale, logit_bias, pair_index):
    own_images = image_embed.shape[0]
    rings = image_rings()
    images = lax.all_gather(image_embed, AXES, axis=0, tiled=True, axis_index_groups=rings)

    texts = spread(text_packets(pair_index, text_embed, lax.axis_size("z")), "z")
    own = spread(jnp.broadcast_to(texts[None], (lax.axis_size("x"),) + texts.shape), "x")
    other = exchanged(own)

    scale = jnp.exp(log_scale)
    scalars = jnp.concatenate([scale, -math.log2(math.e) * scale, -math.log2(math.e) * logit_bias])
    z, x, c = lax.axis_index("z"), lax.axis_index("x"), lax.axis_index("c")
    place = jnp.arange(SIZES[1], dtype=jnp.int32)
    place = jnp.where(c == 0, place, SIZES[1] - 1 - place)
    first = (((z * SIZES[1] + place) * SIZES[2] + x) * SIZES[3] + c) * own_images

    image_part, own_part, other_part = pair_terms(first.astype(jnp.int32), scalars, images, own, other)
    image_grad = lax.psum_scatter(image_part, AXES, scatter_dimension=0, tiled=True, axis_index_groups=rings)

    text_part = own_part.astype(jnp.float32) + exchanged(other_part).astype(jnp.float32)
    text_part = jnp.sum(parted(text_part.astype(jnp.bfloat16), "x").astype(jnp.float32), axis=0)
    text_grads = parted(text_part.astype(jnp.bfloat16), "z")
    return unit_backward(image_embed, text_embed, image_grad, text_grads)


def solution(mesh):
    split = Mesh(mesh.devices.reshape(SIZES), AXES)
    rows = P(AXES, None)
    return jax.shard_map(
        on_device,
        mesh=split,
        in_specs=(rows, rows, P(), P(), P(AXES)),
        out_specs=(rows, rows),
        check_vma=False,
    )
```
